32 devices in a mesh: wide: 16 (over z, y, x), narrow: 2 (over core).
Axes of the slice: x: 2, y: 2, z: 4, core: 2. Of those that a mesh axis runs over, the one named last changes fastest.
Arguments:
- rhs: float32 [256, 32, 128], P('wide', 'narrow'), may hold values from -4 to 4
- alpha: float32 [256, 32, 128], P('wide', 'narrow'), may hold values from 0.05 to 0.5
- beta: float32 [256, 32, 128], P('wide', 'narrow'), may hold values from 0.5 to 4
Outputs:
- solution: float32 [256, 32, 128], P('wide', 'narrow')
The draws below stay inside these ranges and needn't reach their ends.
All inputs are finite; a program needn't handle non-finite values.
Results may differ from the reference program's by a relative error of at most 0.00002.
Values sent between devices are 32-bit elements; how exact they have to be, the bound alone decides.
No kernel may reach another device: no remote copies, remote signals or barrier semaphores. Data moves between devices by JAX's collectives and lax.ppermute only.
A program may use at most 64 MiB of HBM per device.

```python
import math
import jax
import jax.numpy as jnp

NY = 128
LEVELS = 6
SWEEPS = 2
BOTTOM = 6
NX = 256
NZ = 32


def draw_rhs(key, part):
    key = jax.random.fold_in(key, 7)
    shape = (NX, NZ, NY)
    return jnp.clip(jax.random.normal(key, shape, jnp.float32), -4.0, 4.0)


def levels(rng, dims, cuts, low, high):
    factor_of, own = 1.0, jax.random.fold_in(rng, 6)
    for dim, parts in cuts:
        steps = jnp.exp(jax.random.uniform(jax.random.fold_in(own, dim), (parts,), jnp.float32, low / len(cuts), high / len(cuts)))
        factor_of = factor_of * jnp.repeat(steps, dims[dim] // parts).reshape([-1 if axis == dim else 1 for axis in range(len(dims))])
    return factor_of


def setup_inputs(seed: int = 0) -> dict:
    streams_of = jax.random.split(jax.random.key(seed), 4)
    rhs = draw_rhs(jax.random.fold_in(streams_of[3], 71), 0)
    alpha = jnp.clip(jnp.exp(math.log(0.5) - 2.3025851 * jax.random.uniform(streams_of[1], (NX, NZ, NY), jnp.float32) ** levels(streams_of[1], (NX, NZ, NY), ((0, 16), (1, 2)), -0.2, 0.2)), 0.05, 0.5)
    beta = jnp.clip(jnp.exp(math.log(4.0) - 2.0794415 * jax.random.uniform(streams_of[2], (NX, NZ, NY), jnp.float32) ** levels(streams_of[2], (NX, NZ, NY), ((0, 16), (1, 2)), -0.2, 0.2)), 0.5, 4.0)
    return dict(rhs=rhs, alpha=alpha, beta=beta)


OMEGA = 2.0 / 3.0


def extend_xz(grid_field):
    return jnp.pad(grid_field, ((1, 1), (1, 1), (0, 0)))


def neighbours(extended):
    centre = extended[1:-1, 1:-1]
    padded_y = jnp.pad(centre, ((0, 0), (0, 0), (1, 1)))
    return (extended[:-2, 1:-1], extended[2:, 1:-1], extended[1:-1, :-2], extended[1:-1, 2:], padded_y[:, :, :-2], padded_y[:, :, 2:])


def level_setup(alpha_grid, beta_ext, factor):
    beta_grid = beta_ext[1:-1, 1:-1]
    couple = tuple(0.5 * (beta_grid + other_cell) for other_cell in neighbours(beta_ext))
    diagonal = alpha_grid + factor * (couple[0] + couple[1] + couple[2] + couple[3] + couple[4] + couple[5])
    return couple, diagonal


def apply_operator(extended, couple, diagonal, factor):
    nearby = neighbours(extended)
    total = couple[0] * nearby[0] + couple[1] * nearby[1] + couple[2] * nearby[2]
    total = total + couple[3] * nearby[3] + couple[4] * nearby[4] + couple[5] * nearby[5]
    return diagonal * extended[1:-1, 1:-1] - factor * total


def relax_once(iterate, extended, source, couple, diagonal, factor):
    return iterate + OMEGA * (source - apply_operator(extended, couple, diagonal, factor)) / diagonal


def restrict(grid_field):
    half_x = grid_field.shape[0] // 2
    half_z = grid_field.shape[1] // 2
    half_y = grid_field.shape[2] // 2
    return grid_field.reshape(half_x, 2, half_z, 2, half_y, 2).sum(axis=(1, 3, 5)) * 0.125


def prolong(grid_field):
    return jnp.repeat(jnp.repeat(jnp.repeat(grid_field, 2, axis=0), 2, axis=1), 2, axis=2)


def coarse_cycle(level_index, source, alpha_grid, beta_grid):
    factor = 0.25 ** level_index
    couple, diagonal = level_setup(alpha_grid, extend_xz(beta_grid), factor)
    iterate = OMEGA * source / diagonal
    if level_index == LEVELS - 1:
        for sweep_index in range(BOTTOM - 1):
            iterate = relax_once(iterate, extend_xz(iterate), source, couple, diagonal, factor)
        return iterate
    for sweep_index in range(SWEEPS - 1):
        iterate = relax_once(iterate, extend_xz(iterate), source, couple, diagonal, factor)
    leftover = source - apply_operator(extend_xz(iterate), couple, diagonal, factor)
    correct = coarse_cycle(level_index + 1, restrict(leftover), restrict(alpha_grid), restrict(beta_grid))
    iterate = iterate + prolong(correct)
    for sweep_index in range(SWEEPS):
        iterate = relax_once(iterate, extend_xz(iterate), source, couple, diagonal, factor)
    return iterate


def reference(rhs, alpha, beta):
    return coarse_cycle(0, rhs, alpha, beta)
```

```python
import functools
import math

import jax
import jax.numpy as jnp
from jax import lax
from jax.experimental import pallas as pl
from jax.experimental.pallas import tpu as pltpu
from jax.sharding import PartitionSpec as P

LEVELS = 6
BOTTOM = 6
OMEGA = 2.0 / 3.0
LANES = 128
H = 11
H1 = 5
LONGEST = 2048


def short(n, rows):
    return n * rows <= LONGEST


def each(n, rows, body):
    if short(n, rows):
        for i in range(n):
            body(i)
    else:

        def step(i, _):
            body(i)
            return 0

        lax.fori_loop(0, n, step, 0)


F, W, CX, CZ, CY, U, A, B, V = range(9)
KEPT = 6


class Level:
    def __init__(self, ref, zw, index, base=0):
        self.ref, self.zw, self.base = ref, zw, base
        self.d, self.s = 2**index, 0.25**index

    def at(self, plane):
        return Level.moved(self, self.base + plane * self.zw)

    def moved(self, base):
        other = Level(self.ref, self.zw, 0, base)
        other.d, other.s = self.d, self.s
        return other

    def get(self, q, r, n):
        return self.ref[q, pl.ds(r, n), :]

    def put(self, q, r, value):
        self.ref[q, pl.ds(r, value.shape[0]), :] = value

    def setup(self, first, count, chunk, valid=None):
        zw, d = self.zw, self.d
        n = chunk * zw
        row = lax.broadcasted_iota(jnp.int32, (n, LANES), 0) % zw
        lane = lax.broadcasted_iota(jnp.int32, (n, LANES), 1)
        z0, z1, y0, y1 = row == 0, row == zw - 1, lane < d, lane >= LANES - d
        hs = 0.5 * self.s

        def body(i):
            p = first + i * chunk
            r = self.base + p * zw
            b = self.get(B, r, n)
            bxp = self.get(B, r + zw, n)
            bxm = self.get(B, r - zw, n)
            bzp = jnp.where(z1, 0.0, self.get(B, r + 1, n))
            bzm = jnp.where(z0, 0.0, self.get(B, r - 1, n))
            byp = jnp.where(y1, 0.0, pltpu.roll(b, LANES - d, 1))
            bym = jnp.where(y0, 0.0, pltpu.roll(b, d, 1))
            dg = self.get(A, r, n) + hs * (6.0 * b + bxp + bxm + bzp + bzm + byp + bym)
            w = OMEGA / dg
            if valid is not None:
                w = jnp.where(valid(p), w, 0.0)
            self.put(A, r, dg)
            self.put(W, r, w)
            self.put(U, r, w * self.get(F, r, n))
            self.put(CX, r, hs * (b + bxp))
            self.put(CZ, r, jnp.where(z1, 0.0, hs * (b + bzp)))
            self.put(CY, r, jnp.where(y1, 0.0, hs * (b + byp)))

        assert count % chunk == 0
        each(count // chunk, n, body)

    def first_cx(self, plane):
        r = self.base + plane * self.zw
        n = self.zw
        self.put(CX, r, (0.5 * self.s) * (self.get(B, r, n) + self.get(B, r + n, n)))

    def around(self, q, r, n):
        zw, d = self.zw, self.d
        v = self.get(q, r, n)
        t = self.get(CX, r, n) * self.get(q, r + zw, n)
        t = t + self.get(CX, r - zw, n) * self.get(q, r - zw, n)
        t = t + self.get(CZ, r, n) * self.get(q, r + 1, n)
        t = t + self.get(CZ, r - 1, n) * self.get(q, r - 1, n)
        cy = self.get(CY, r, n)
        t = t + cy * pltpu.roll(v, LANES - d, 1)
        t = t + pltpu.roll(cy * v, d, 1)
        return v, t

    def sweep(self, src, dst, first, count, chunk):
        n = chunk * self.zw

        def body(i):
            r = self.base + (first + i * chunk) * self.zw
            v, t = self.around(src, r, n)
            self.put(dst, r, (1.0 - OMEGA) * v + self.get(W, r, n) * (self.get(F, r, n) + t))

        assert count % chunk == 0
        each(count // chunk, n, body)

    def residual(self, q, r, n):
        v, t = self.around(q, r, n)
        return self.get(F, r, n) + t - self.get(A, r, n) * v


def lane_pairs(t, d):
    s = t + pltpu.roll(t, LANES - d, 1)
    lane = lax.broadcasted_iota(jnp.int32, t.shape, 1)
    return jnp.where((lane // d) % 2 == 0, s, pltpu.roll(s, d, 1))


def restrict_planes(get, fine, first, pairs, coarse, q, plane, tmp, per):
    zw = fine.zw
    half = zw // 2

    def body(i):
        r = fine.base + (first + 2 * i * per) * zw
        t0 = i * per * zw if short(pairs // per, 2 * per * zw) else 0
        for k in range(per):
            v = get(r + 2 * k * zw, 2 * zw)
            tmp[pl.ds(t0 + k * zw, zw), :] = v[:zw] + v[zw:]
        t = tmp[pl.ds(t0, per * half, 2), :] + tmp[pl.ds(t0 + 1, per * half, 2), :]
        coarse.put(q, coarse.base + plane * half + i * per * half, lane_pairs(t, fine.d) * 0.125)

    assert pairs % per == 0
    each(pairs // per, 2 * per * zw, body)


def restrict_small(value, fine, coarse, q, tmp, count):
    zw, zc = fine.zw, coarse.zw
    tmp[pl.ds(0, count * 2 * zw), :] = value
    for z in range(zc):
        t = None
        for dx in range(2):
            for dz in range(2):
                part = tmp[pl.ds(dx * zw + 2 * z + dz, count, 2 * zw), :]
                t = part if t is None else t + part
        t = lane_pairs(t, fine.d) * 0.125
        if zc == 1:
            coarse.put(q, coarse.base, t)
        else:
            coarse.ref[q, pl.ds(coarse.base + z, count, zc), :] = t


def prolong_small(coarse, q, fine, p, tmp, count):
    zw, zc = fine.zw, coarse.zw
    for z in range(zc):
        v = coarse.get(q, coarse.base, count) if zc == 1 else coarse.ref[q, pl.ds(coarse.base + z, count, zc), :]
        for dx in range(2):
            for dz in range(2):
                tmp[pl.ds(dx * zw + 2 * z + dz, count, 2 * zw), :] = v
    n = count * 2 * zw
    fine.put(p, fine.base, fine.get(p, fine.base, n) + tmp[pl.ds(0, n), :])


def prolong_planes(coarse, q, plane, count, fine, src, dst, first, tmp, per=1):
    zw = fine.zw
    half = zw // 2

    def body(i):
        v = coarse.get(q, coarse.base + (plane + i * per) * half, per * half)
        t0 = i * per * zw if short(count // per, 2 * per * zw) else 0
        tmp[pl.ds(t0, per * half, 2), :] = v
        tmp[pl.ds(t0 + 1, per * half, 2), :] = v
        for k in range(per):
            e = tmp[pl.ds(t0 + k * zw, zw), :]
            r = fine.base + (first + 2 * (i * per + k)) * zw
            fine.put(dst, r, fine.get(src, r, zw) + e)
            fine.put(dst, r + zw, fine.get(src, r + zw, zw) + e)

    assert count % per == 0
    each(count // per, 2 * per * zw, body)


def keep(level, q, first, count, dst, k, sem):
    src = level.ref.at[q, pl.ds(first * level.zw, count * level.zw)]
    copy = pltpu.make_async_copy(src, dst.at[k], sem.at[k])
    copy.start()
    return copy


def down_kernel(
    bx, bz, n_wide, n_narrow, rhs, alpha, beta, lo, hi, other, packed, keep0, keep1, lev0, lev1, part, tmp, sem0, sem1
):
    zw = bz * n_narrow
    planes = bx + 2 * H
    wide = lax.axis_index("wide")
    narrow = lax.axis_index("narrow")
    l0 = Level(lev0, zw, 0)
    l1 = Level(lev1, zw // 2, 1)

    def place(q, src, src_plane, count, plane, z):
        def body(i):
            r = pl.multiple_of((plane + i) * zw + z, 8)
            l0.put(q, r, src[pl.ds((src_plane + i) * bz, bz), :])

        each(count, bz, body)

    g = H - 1
    all_h = 2 * g + H
    total = 3 * bx + 2 * all_h
    for q, own, at, size in ((F, rhs, 0, g), (A, alpha, g, g), (B, beta, 2 * g, H)):
        place(q, lo, at, size, H - size, narrow * bz)
        place(q, own, 0, bx, H, narrow * bz)
        place(q, hi, at, size, H + bx, narrow * bz)
        for k in range(n_narrow - 1):
            z = (1 - narrow if n_narrow == 2 else lax.rem(narrow + 1 + k, n_narrow)) * bz
            o = k * total + 3 * bx
            place(q, other, k * total + (F, A, B).index(q) * bx, bx, H, z)
            place(q, other, o + at, size, H - size, z)
            place(q, other, o + all_h + at, size, H + bx, z)
    first0, count0 = H - 2, bx + 4
    p1 = bx // 2 + 2 * H1
    waits = [keep(l0, F, first0, count0, keep0, F, sem0)]

    def valid0(p):
        x = wide * bx - H + p
        return jnp.logical_and(x >= 0, x < n_wide * bx)

    restrict_planes(lambda r, n: l0.get(B, r, n), l0, 1, p1, l1, B, 0, tmp.at[0], 1)
    restrict_planes(lambda r, n: l0.get(A, r, n), l0, 3, p1 - 2, l1, A, 1, tmp.at[1], 1)
    l0.first_cx(0)
    l0.setup(1, planes - 2, 1, valid0)
    waits += [keep(l0, q, first0, count0, keep0, q, sem0) for q in (W, CX, CZ, CY)]
    l0.sweep(U, V, 2, planes - 4, 1)
    waits.append(keep(l0, V, first0, count0, keep0, U, sem0))
    restrict_planes(lambda r, n: l0.residual(V, r, n), l0, 3, p1 - 2, l1, F, 1, tmp.at[2], 1)

    def valid1(p):
        x = wide * (bx // 2) - H1 + p
        return jnp.logical_and(x >= 0, x < n_wide * (bx // 2))

    k2 = bx // 4
    z2 = zw // 4
    n2 = k2 * z2
    l2 = Level(part, z2, 2)
    restrict_planes(lambda r, n: l1.get(A, r, n), l1, H1, k2, l2, 1, 0, tmp.at[1], 1)
    restrict_planes(lambda r, n: l1.get(B, r, n), l1, H1, k2, l2, 2, 0, tmp.at[0], 1)
    l1.first_cx(0)
    l1.setup(1, p1 - 2, 1, valid1)
    l1.sweep(U, V, 2, p1 - 4, 1)
    waits += [keep(l1, q, 1, p1 - 2, keep1, q, sem1) for q in (F, W, CX, CZ, CY)]
    waits.append(keep(l1, V, 1, p1 - 2, keep1, U, sem1))
    restrict_planes(lambda r, n: l1.residual(V, r, n), l1, H1, k2, l2, 0, 0, tmp.at[2], 1)
    which = lax.broadcasted_iota(jnp.int32, (n2, LANES), 1) % 4
    packed[...] = jnp.where(which == 0, part[0], jnp.where(which == 1, part[1], part[2]))
    for copy in waits:
        copy.wait()


def margin(zl, index):
    return max(8, (4 if index == 2 else 2) * zl)


def up_kernel(
    bx, bz, n_wide, n_narrow, gathered, keep0, keep1, out, lev2, lev3, lev4, lev5, lev0, lev1, tmp, sem, sem0, sem1
):
    wide = lax.axis_index("wide")
    narrow = lax.axis_index("narrow")
    zw = bz * n_narrow
    fetch = []
    for kept, lev, done in ((keep1, lev1, sem1), (keep0, lev0, sem0)):
        for q in range(KEPT):
            copy = pltpu.make_async_copy(kept.at[q], lev.at[q], done.at[q])
            copy.start()
            fetch.append(copy)
    m = margin(zw // 4, 2)
    arrive = pltpu.make_async_copy(gathered, lev2.at[U, pl.ds(m, n_wide * bx // 4 * (zw // 4))], sem)
    arrive.start()
    levels = []
    for index, ref in enumerate((lev2, lev3, lev4, lev5), 2):
        zl = zw // 2**index
        m = margin(zl, index)
        level = Level(ref, zl, index, m)
        level.nx = n_wide * bx // 2**index
        levels.append(level)
        zero = jnp.zeros((m, LANES), jnp.float32)
        for q in (F, W, CX, CZ, CY, U, B):
            level.put(q, 0, zero)
            level.put(q, m + level.nx * zl, zero)
    l2, l3, l4, l5 = levels
    planes2 = bx // 4
    n = planes2 * l2.zw
    lane = lax.broadcasted_iota(jnp.int32, (n, LANES), 1) % 4

    def unpack(i):
        p = l2.get(U, l2.base + i * n, n)
        for q, k, first, second in ((F, 0, 1, 2), (A, 1, LANES - 1, 2), (B, 2, 1, LANES - 2)):
            t = jnp.where(lane == k, p, 0.0)
            t = t + pltpu.roll(t, first, 1)
            t = t + pltpu.roll(t, second, 1)
            l2.put(q, l2.base + i * n, t)

    arrive.wait()
    each(n_wide, n, unpack)

    def chunk_of(level):
        return max(1, min(32 // level.zw, level.nx))

    def down(level, coarse, q, get, t):
        if level.zw >= 8:
            restrict_planes(get, level, 0, coarse.nx, coarse, q, 0, t, max(1, 16 // level.zw))
        else:
            restrict_small(get(level.base, level.nx * level.zw), level, coarse, q, t, coarse.nx)

    for level, coarse in ((l2, l3), (l3, l4), (l4, l5)):
        down(level, coarse, A, lambda r, m, level=level: level.get(A, r, m), tmp.at[0])
        down(level, coarse, B, lambda r, m, level=level: level.get(B, r, m), tmp.at[1])
    for level, coarse in ((l2, l3), (l3, l4), (l4, l5)):
        level.setup(0, level.nx, chunk_of(level))
        level.sweep(U, B, 0, level.nx, chunk_of(level))
        down(level, coarse, F, lambda r, m, level=level: level.residual(B, r, m), tmp.at[2])
    l5.setup(0, l5.nx, chunk_of(l5))
    src, dst = U, B
    for _ in range(BOTTOM - 1):
        l5.sweep(src, dst, 0, l5.nx, chunk_of(l5))
        src, dst = dst, src
    coarse = l5
    for level in (l4, l3):
        if level.zw >= 8:
            prolong_planes(coarse, src, 0, coarse.nx, level, B, B, 0, tmp.at[0], max(1, 16 // level.zw))
        else:
            prolong_small(coarse, src, level, B, tmp.at[0], coarse.nx)
        level.sweep(B, U, 0, level.nx, chunk_of(level))
        level.sweep(U, B, 0, level.nx, chunk_of(level))
        coarse, src = level, B
    start = wide * planes2
    r2 = pl.multiple_of(l2.base + start * l2.zw, 8)
    near2 = l2.moved(r2)
    near3 = l3.moved(l3.base + (start // 2) * l3.zw)
    prolong_planes(near3, B, -2, planes2 // 2 + 4, near2, B, B, -4, tmp.at[1], 2 if l2.zw < 16 else 1)
    near2.sweep(B, U, -3, planes2 + 6, 2)
    near2.sweep(U, B, -2, planes2 + 4, 2)
    for copy in fetch:
        copy.wait()
    l1 = Level(lev1, zw // 2, 1)
    count1 = bx // 2 + 2 * H1 - 2
    prolong_planes(near2, B, -2, count1 // 2, l1, U, U, 0, tmp.at[0])
    l1.sweep(U, KEPT, 2, count1 - 4, 1)
    l1.sweep(KEPT, U, 3, count1 - 6, 1)
    l0 = Level(lev0, zw, 0)
    prolong_planes(l1, U, 3, bx // 2 + 2, l0, U, U, 0, tmp.at[1])
    l0.sweep(U, KEPT, 1, bx + 2, 1)
    l0.sweep(KEPT, U, 2, bx, 1)

    def give(i):
        r = pl.multiple_of((2 + i) * zw + narrow * bz, 8)
        out[pl.ds(i * bz, bz), :] = l0.get(U, r, bz)

    each(bx, bz, give)


def shift(array, by):
    n = lax.axis_size("wide")
    return lax.ppermute(array, "wide", [(i, i + by) for i in range(n) if 0 <= i + by < n])


def shards(n_wide, n_narrow, rhs, alpha, beta):
    bx, bz, lanes = rhs.shape
    g = H - 1
    lo = shift(jnp.concatenate([rhs[bx - g :], alpha[bx - g :], beta[bx - H :]]), 1)
    hi = shift(jnp.concatenate([rhs[:g], alpha[:g], beta[:H]]), -1)
    bundle = jnp.concatenate([rhs, alpha, beta, lo, hi])
    if n_narrow == 2:
        other = lax.ppermute(bundle, "narrow", [(0, 1), (1, 0)])
    else:
        other = jnp.concatenate(
            [
                lax.ppermute(bundle, "narrow", [((i + k) % n_narrow, i) for i in range(n_narrow)])
                for k in range(1, n_narrow)
            ]
        )
    flat = lambda t: t.reshape(-1, lanes)
    zw = bz * n_narrow
    f32 = jnp.float32
    planes, p1 = bx + 2 * H, bx // 2 + 2 * H1
    n2 = (bx // 4) * (zw // 4)
    vmem, hbm = pl.BlockSpec(memory_space=pltpu.VMEM), pl.BlockSpec(memory_space=pl.ANY)
    keep0 = jax.ShapeDtypeStruct((KEPT, (bx + 4) * zw, lanes), f32)
    keep1 = jax.ShapeDtypeStruct((KEPT, (p1 - 2) * (zw // 2), lanes), f32)
    sems = [pltpu.SemaphoreType.DMA((KEPT,)), pltpu.SemaphoreType.DMA((KEPT,))]

    def params(scratch, rows):
        size = 4 * sum(math.prod(t.shape) for t in scratch[:-2]) + 4 * lanes * rows
        return pltpu.CompilerParams(vmem_limit_bytes=min(63 * 2**20, size + size // 8 + 2**21))

    scratch = [
        pltpu.VMEM((9, planes * zw, lanes), f32),
        pltpu.VMEM((9, p1 * (zw // 2), lanes), f32),
        pltpu.VMEM((3, n2, lanes), f32),
        pltpu.VMEM((3, p1 * zw, lanes), f32),
        *sems,
    ]
    packed, keep0, keep1 = pl.pallas_call(
        functools.partial(down_kernel, bx, bz, n_wide, n_narrow),
        out_shape=[jax.ShapeDtypeStruct((n2, lanes), f32), keep0, keep1],
        in_specs=[vmem] * 6,
        out_specs=[vmem, hbm, hbm],
        scratch_shapes=scratch,
        compiler_params=params(scratch, 3 * planes * zw),
        name="down",
    )(flat(rhs), flat(alpha), flat(beta), flat(lo), flat(hi), flat(other))
    gathered = lax.all_gather(packed, "wide", tiled=True)
    nx = n_wide * bx
    scratch = []
    for index in range(2, LEVELS):
        zl = zw // 2**index
        scratch.append(pltpu.VMEM((8, nx // 2**index * zl + 2 * margin(zl, index), lanes), f32))
    scratch += [
        pltpu.VMEM((KEPT + 1, *keep0.shape[1:]), f32),
        pltpu.VMEM((KEPT + 1, *keep1.shape[1:]), f32),
        pltpu.VMEM((3, max((bx // 2 + 2) * zw, LONGEST // 2), lanes), f32),
        pltpu.SemaphoreType.DMA,
        *sems,
    ]
    out = pl.pallas_call(
        functools.partial(up_kernel, bx, bz, n_wide, n_narrow),
        out_shape=jax.ShapeDtypeStruct((bx * bz, lanes), f32),
        in_specs=[hbm] * 3,
        out_specs=vmem,
        scratch_shapes=scratch,
        compiler_params=params(scratch[:-3] + sems, bx * bz),
        name="up",
    )(gathered, keep0, keep1)
    return out.reshape(bx, bz, lanes)


def solution(mesh):
    n_wide, n_narrow = mesh.shape["wide"], mesh.shape["narrow"]
    spec = P("wide", "narrow", None)
    return jax.shard_map(
        functools.partial(shards, n_wide, n_narrow),
        mesh=mesh,
        in_specs=(spec, spec, spec),
        out_specs=spec,
        check_vma=False,
    )
```

```python
import functools
import math

import jax
import jax.numpy as jnp
from jax import lax
from jax.experimental import pallas as pl
from jax.experimental.pallas import tpu as pltpu
from jax.sharding import PartitionSpec as P

LEVELS = 6
BOTTOM = 6
OMEGA = 2.0 / 3.0
LANES = 128
H1 = 3
H = 2 * H1 + 1
LONGEST = 2048


def short(n, rows):
    return n * rows <= LONGEST


def each(n, rows, body):
    if short(n, rows):
        for i in range(n):
            body(i)
    else:

        def step(i, _):
            body(i)
            return 0

        lax.fori_loop(0, n, step, 0)


F, W, CX, CZ, CY, U, A, B, V = range(9)
KEPT = 6


class Level:
    def __init__(self, ref, zw, index, base=0):
        self.ref, self.zw, self.base = ref, zw, base
        self.d, self.s = 2**index, 0.25**index

    def at(self, plane):
        return Level.moved(self, self.base + plane * self.zw)

    def moved(self, base):
        other = Level(self.ref, self.zw, 0, base)
        other.d, other.s = self.d, self.s
        return other

    def get(self, q, r, n):
        return self.ref[q, pl.ds(r, n), :]

    def put(self, q, r, value):
        self.ref[q, pl.ds(r, value.shape[0]), :] = value

    def setup(self, first, count, chunk, valid=None):
        zw, d = self.zw, self.d
        n = chunk * zw
        row = lax.broadcasted_iota(jnp.int32, (n, LANES), 0) % zw
        lane = lax.broadcasted_iota(jnp.int32, (n, LANES), 1)
        z0, z1, y0, y1 = row == 0, row == zw - 1, lane < d, lane >= LANES - d
        hs = 0.5 * self.s

        def body(i):
            p = first + i * chunk
            r = self.base + p * zw
            b = self.get(B, r, n)
            bxp = self.get(B, r + zw, n)
            bxm = self.get(B, r - zw, n)
            bzp = jnp.where(z1, 0.0, self.get(B, r + 1, n))
            bzm = jnp.where(z0, 0.0, self.get(B, r - 1, n))
            byp = jnp.where(y1, 0.0, pltpu.roll(b, LANES - d, 1))
            bym = jnp.where(y0, 0.0, pltpu.roll(b, d, 1))
            dg = self.get(A, r, n) + hs * (6.0 * b + bxp + bxm + bzp + bzm + byp + bym)
            w = OMEGA / dg
            if valid is not None:
                w = jnp.where(valid(p), w, 0.0)
            self.put(A, r, dg)
            self.put(W, r, w)
            self.put(U, r, w * self.get(F, r, n))
            self.put(CX, r, hs * (b + bxp))
            self.put(CZ, r, jnp.where(z1, 0.0, hs * (b + bzp)))
            self.put(CY, r, jnp.where(y1, 0.0, hs * (b + byp)))

        assert count % chunk == 0
        each(count // chunk, n, body)

    def first_cx(self, plane):
        r = self.base + plane * self.zw
        n = self.zw
        self.put(CX, r, (0.5 * self.s) * (self.get(B, r, n) + self.get(B, r + n, n)))

    def around(self, q, r, n):
        zw, d = self.zw, self.d
        v = self.get(q, r, n)
        t = self.get(CX, r, n) * self.get(q, r + zw, n)
        t = t + self.get(CX, r - zw, n) * self.get(q, r - zw, n)
        t = t + self.get(CZ, r, n) * self.get(q, r + 1, n)
        t = t + self.get(CZ, r - 1, n) * self.get(q, r - 1, n)
        cy = self.get(CY, r, n)
        t = t + cy * pltpu.roll(v, LANES - d, 1)
        t = t + pltpu.roll(cy * v, d, 1)
        return v, t

    def sweep(self, src, dst, first, count, chunk):
        n = chunk * self.zw

        def body(i):
            r = self.base + (first + i * chunk) * self.zw
            v, t = self.around(src, r, n)
            self.put(dst, r, (1.0 - OMEGA) * v + self.get(W, r, n) * (self.get(F, r, n) + t))

        assert count % chunk == 0
        each(count // chunk, n, body)

    def residual(self, q, r, n):
        v, t = self.around(q, r, n)
        return self.get(F, r, n) + t - self.get(A, r, n) * v


def lane_pairs(t, d):
    s = t + pltpu.roll(t, LANES - d, 1)
    lane = lax.broadcasted_iota(jnp.int32, t.shape, 1)
    return jnp.where((lane // d) % 2 == 0, s, pltpu.roll(s, d, 1))


def restrict_planes(get, fine, first, pairs, coarse, q, plane, tmp, per):
    zw = fine.zw
    half = zw // 2

    def body(i):
        r = fine.base + (first + 2 * i * per) * zw
        t0 = i * per * zw if short(pairs // per, 2 * per * zw) else 0
        for k in range(per):
            v = get(r + 2 * k * zw, 2 * zw)
            tmp[pl.ds(t0 + k * zw, zw), :] = v[:zw] + v[zw:]
        t = tmp[pl.ds(t0, per * half, 2), :] + tmp[pl.ds(t0 + 1, per * half, 2), :]
        coarse.put(q, coarse.base + plane * half + i * per * half, lane_pairs(t, fine.d) * 0.125)

    assert pairs % per == 0
    each(pairs // per, 2 * per * zw, body)


def restrict_small(value, fine, coarse, q, tmp, count):
    zw, zc = fine.zw, coarse.zw
    tmp[pl.ds(0, count * 2 * zw), :] = value
    for z in range(zc):
        t = None
        for dx in range(2):
            for dz in range(2):
                part = tmp[pl.ds(dx * zw + 2 * z + dz, count, 2 * zw), :]
                t = part if t is None else t + part
        t = lane_pairs(t, fine.d) * 0.125
        if zc == 1:
            coarse.put(q, coarse.base, t)
        else:
            coarse.ref[q, pl.ds(coarse.base + z, count, zc), :] = t


def prolong_small(coarse, q, fine, p, tmp, count):
    zw, zc = fine.zw, coarse.zw
    for z in range(zc):
        v = coarse.get(q, coarse.base, count) if zc == 1 else coarse.ref[q, pl.ds(coarse.base + z, count, zc), :]
        for dx in range(2):
            for dz in range(2):
                tmp[pl.ds(dx * zw + 2 * z + dz, count, 2 * zw), :] = v
    n = count * 2 * zw
    fine.put(p, fine.base, fine.get(p, fine.base, n) + tmp[pl.ds(0, n), :])


def prolong_planes(coarse, q, plane, count, fine, src, dst, first, tmp, per=1):
    zw = fine.zw
    half = zw // 2

    def body(i):
        v = coarse.get(q, coarse.base + (plane + i * per) * half, per * half)
        t0 = i * per * zw if short(count // per, 2 * per * zw) else 0
        tmp[pl.ds(t0, per * half, 2), :] = v
        tmp[pl.ds(t0 + 1, per * half, 2), :] = v
        for k in range(per):
            e = tmp[pl.ds(t0 + k * zw, zw), :]
            r = fine.base + (first + 2 * (i * per + k)) * zw
            fine.put(dst, r, fine.get(src, r, zw) + e)
            fine.put(dst, r + zw, fine.get(src, r + zw, zw) + e)

    assert count % per == 0
    each(count // per, 2 * per * zw, body)


def keep(level, q, first, count, dst, k, sem):
    src = level.ref.at[q, pl.ds(first * level.zw, count * level.zw)]
    copy = pltpu.make_async_copy(src, dst.at[k], sem.at[k])
    copy.start()
    return copy


def rev(x, bits):
    return sum(((x >> k) & 1) << (bits - 1 - k) for k in range(bits)) if bits else 0


def bits_of(n):
    return n.bit_length() - 1


def pack_kernel(bx, bz, rhs, alpha, beta, even, odd, own, sem):
    up = 1 - lax.axis_index("wide") % 2
    waits = []
    at = [0, 0]
    for q, (src, size) in enumerate(((rhs, H - 1), (alpha, H - 1), (beta, H))):
        for k, dst in enumerate((even, odd)):
            upper = up if k == 0 else 1 - up
            start = pl.multiple_of(upper * ((bx - size) * bz), 8)
            copy = pltpu.make_async_copy(
                src.at[pl.ds(start, size * bz)], dst.at[pl.ds(at[k] * bz, size * bz)], sem.at[2 * q + k]
            )
            copy.start()
            waits.append(copy)
            at[k] += size
        copy = pltpu.make_async_copy(src, own.at[pl.ds(q * bx * bz, bx * bz)], sem.at[6 + q])
        copy.start()
        waits.append(copy)
    for copy in waits:
        copy.wait()


def down_kernel(
    bx, bz, n_wide, n_narrow, own, even, odd, other, others, packed, ueven, uodd, keep0, keep1, lev0, lev1, part, tmp, sem0, sem1
):
    zw = bz * n_narrow
    planes = bx + 2 * H
    wide = lax.axis_index("wide")
    narrow = lax.axis_index("narrow")
    up = 1 - wide % 2
    l0 = Level(lev0, zw, 0)
    l1 = Level(lev1, zw // 2, 1)

    def place(q, src, src_plane, count, plane, z):
        def body(i):
            r = pl.multiple_of((plane + i) * zw + z, 8)
            l0.put(q, r, src[pl.ds((src_plane + i) * bz, bz), :])

        each(count, bz, body)

    g = H - 1
    all_h = 2 * g + H
    for index, (q, at, size) in enumerate(((F, 0, g), (A, g, g), (B, 2 * g, H))):
        above, below = H + bx, H - size
        p_even = up * above + (1 - up) * below
        p_odd = (1 - up) * above + up * below
        place(q, own, index * bx, bx, H, narrow * bz)
        place(q, even, at, size, p_even, narrow * bz)
        place(q, odd, at, size, p_odd, narrow * bz)
        for k in range(n_narrow - 1):
            z = (1 - narrow if n_narrow == 2 else lax.rem(narrow + 1 + k, n_narrow)) * bz
            place(q, other, (3 * k + index) * bx, bx, H, z)
            place(q, others, 2 * k * all_h + at, size, p_even, z)
            place(q, others, (2 * k + 1) * all_h + at, size, p_odd, z)
    first0, count0 = H - 2, bx + 4
    p1 = bx // 2 + 2 * H1
    waits = [keep(l0, F, first0, count0, keep0, F, sem0)]

    def valid0(p):
        x = wide * bx - H + p
        return jnp.logical_and(x >= 0, x < n_wide * bx)

    restrict_planes(lambda r, n: l0.get(B, r, n), l0, 1, p1, l1, B, 0, tmp.at[0], 1)
    restrict_planes(lambda r, n: l0.get(A, r, n), l0, 3, p1 - 2, l1, A, 1, tmp.at[1], 1)
    l0.first_cx(0)
    l0.setup(1, planes - 2, 1, valid0)
    waits += [keep(l0, q, first0, count0, keep0, q, sem0) for q in (W, CX, CZ, CY)]
    l0.sweep(U, V, 2, planes - 4, 1)
    waits.append(keep(l0, V, first0, count0, keep0, U, sem0))
    restrict_planes(lambda r, n: l0.residual(V, r, n), l0, 3, p1 - 2, l1, F, 1, tmp.at[2], 1)

    def valid1(p):
        x = wide * (bx // 2) - H1 + p
        return jnp.logical_and(x >= 0, x < n_wide * (bx // 2))

    k2 = bx // 4
    z2 = zw // 4
    n2 = k2 * z2
    l2 = Level(part, z2, 2)
    restrict_planes(lambda r, n: l1.get(A, r, n), l1, H1, k2, l2, 1, 0, tmp.at[1], 1)
    restrict_planes(lambda r, n: l1.get(B, r, n), l1, H1, k2, l2, 2, 0, tmp.at[0], 1)
    l1.first_cx(0)
    l1.put(CZ, 0, jnp.zeros((l1.zw, LANES), jnp.float32))
    l1.setup(1, p1 - 2, 1, valid1)
    l1.sweep(U, V, 2, p1 - 4, 1)
    waits += [keep(l1, q, 0, p1, keep1, q, sem1) for q in (F, W, CX, CZ, CY)]
    waits.append(keep(l1, V, 0, p1, keep1, U, sem1))
    n1 = 2 * l1.zw
    upper, lower = H1 + bx // 2 - 3, H1 + 1
    ueven[...] = l1.get(V, pl.multiple_of((up * upper + (1 - up) * lower) * l1.zw, 8), n1)
    uodd[...] = l1.get(V, pl.multiple_of(((1 - up) * upper + up * lower) * l1.zw, 8), n1)
    restrict_planes(lambda r, n: l1.residual(V, r, n), l1, H1, k2, l2, 0, 0, tmp.at[2], 1)
    which = lax.broadcasted_iota(jnp.int32, (n2, LANES), 1) % 4
    part[0] = jnp.where(which == 0, part[0], jnp.where(which == 1, part[1], part[2]))
    share = n2 // n_narrow
    packed[...] = part[0, pl.ds(pl.multiple_of(narrow * share, 8), share), :]
    for copy in waits:
        copy.wait()


def margin(zl, index):
    return max(8, (4 if index == 2 else 2) * zl)


def up_kernel(
    bx, bz, n_wide, n_narrow, gathered, heven, hodd, keep0, keep1, out, lev2, lev3, lev4, lev5, lev0, lev1, tmp, sem, sem0, sem1
):
    wide = lax.axis_index("wide")
    narrow = lax.axis_index("narrow")
    zw = bz * n_narrow
    fetch = []
    z1 = zw // 2
    for kept, lev, done, r in ((keep1, lev1, sem1, z1), (keep0, lev0, sem0, 0)):
        for q in range(KEPT):
            copy = pltpu.make_async_copy(kept.at[q], lev.at[q, pl.ds(r, kept.shape[1])], done.at[q])
            copy.start()
            fetch.append(copy)
    m = margin(zw // 4, 2)
    arrive = pltpu.make_async_copy(gathered, lev2.at[U, pl.ds(m, n_wide * bx // 4 * (zw // 4))], sem)
    arrive.start()
    levels = []
    for index, ref in enumerate((lev2, lev3, lev4, lev5), 2):
        zl = zw // 2**index
        m = margin(zl, index)
        level = Level(ref, zl, index, m)
        level.nx = n_wide * bx // 2**index
        levels.append(level)
        zero = jnp.zeros((m, LANES), jnp.float32)
        for q in (F, W, CX, CZ, CY, U, B):
            level.put(q, 0, zero)
            level.put(q, m + level.nx * zl, zero)
    l2, l3, l4, l5 = levels
    planes2 = bx // 4
    n2 = planes2 * l2.zw
    n = n2 // n_narrow
    bw, bn = bits_of(n_wide), bits_of(n_narrow)
    me = rev(wide, bw) + n_wide * rev(narrow, bn)
    lane = lax.broadcasted_iota(jnp.int32, (n, LANES), 1) % 4

    def unpack(i):
        w, c = i // n_narrow, i % n_narrow
        at = me ^ (rev(w, bw) + n_wide * rev(c, bn))
        p = l2.get(U, pl.multiple_of(l2.base + at * n, 8), n)
        for q, k, first, second in ((F, 0, 1, 2), (A, 1, LANES - 1, 2), (B, 2, 1, LANES - 2)):
            t = jnp.where(lane == k, p, 0.0)
            t = t + pltpu.roll(t, first, 1)
            t = t + pltpu.roll(t, second, 1)
            l2.put(q, l2.base + i * n, t)

    arrive.wait()
    each(n_wide * n_narrow, n, unpack)

    def chunk_of(level):
        return max(1, min(32 // level.zw, level.nx))

    def down(level, coarse, q, get, t):
        if level.zw >= 8:
            restrict_planes(get, level, 0, coarse.nx, coarse, q, 0, t, max(1, 16 // level.zw))
        else:
            restrict_small(get(level.base, level.nx * level.zw), level, coarse, q, t, coarse.nx)

    for level, coarse in ((l2, l3), (l3, l4), (l4, l5)):
        down(level, coarse, A, lambda r, m, level=level: level.get(A, r, m), tmp.at[0])
        down(level, coarse, B, lambda r, m, level=level: level.get(B, r, m), tmp.at[1])
    for level, coarse in ((l2, l3), (l3, l4), (l4, l5)):
        level.setup(0, level.nx, chunk_of(level))
        level.sweep(U, B, 0, level.nx, chunk_of(level))
        down(level, coarse, F, lambda r, m, level=level: level.residual(B, r, m), tmp.at[2])
    l5.setup(0, l5.nx, chunk_of(l5))
    src, dst = U, B
    for _ in range(BOTTOM - 1):
        l5.sweep(src, dst, 0, l5.nx, chunk_of(l5))
        src, dst = dst, src
    coarse = l5
    for level in (l4, l3):
        if level.zw >= 8:
            prolong_planes(coarse, src, 0, coarse.nx, level, B, B, 0, tmp.at[0], max(1, 16 // level.zw))
        else:
            prolong_small(coarse, src, level, B, tmp.at[0], coarse.nx)
        level.sweep(B, U, 0, level.nx, chunk_of(level))
        level.sweep(U, B, 0, level.nx, chunk_of(level))
        coarse, src = level, B
    start = wide * planes2
    r2 = pl.multiple_of(l2.base + start * l2.zw, 8)
    near2 = l2.moved(r2)
    near3 = l3.moved(l3.base + (start // 2) * l3.zw)
    prolong_planes(near3, B, -2, planes2 // 2 + 4, near2, B, B, -4, tmp.at[1], 2 if l2.zw < 16 else 1)
    near2.sweep(B, U, -3, planes2 + 6, 2)
    near2.sweep(U, B, -2, planes2 + 4, 2)
    for copy in fetch:
        copy.wait()
    l1 = Level(lev1, z1, 1)
    count1 = bx // 2 + 2 * H1 + 2
    up = 1 - wide % 2
    above, below = H1 + bx // 2 + 2, 1
    l1.put(U, pl.multiple_of((up * above + (1 - up) * below) * z1, 8), heven[...])
    l1.put(U, pl.multiple_of(((1 - up) * above + up * below) * z1, 8), hodd[...])
    prolong_planes(near2, B, -2, count1 // 2, l1, U, U, 0, tmp.at[0])
    l1.sweep(U, KEPT, 2, count1 - 4, 1)
    l1.sweep(KEPT, U, 3, count1 - 6, 1)
    l0 = Level(lev0, zw, 0)
    prolong_planes(l1, U, 3, bx // 2 + 2, l0, U, U, 0, tmp.at[1])
    l0.sweep(U, KEPT, 1, bx + 2, 1)
    l0.sweep(KEPT, U, 2, bx, 1)

    def give(i):
        r = pl.multiple_of((2 + i) * zw + narrow * bz, 8)
        out[pl.ds(i * bz, bz), :] = l0.get(U, r, bz)

    each(bx, bz, give)


def swap(array, axis, bit):
    n = lax.axis_size(axis)
    return lax.ppermute(array, axis, [(i, i ^ (1 << bit)) for i in range(n)])


def swap_odd(array):
    n = lax.axis_size("wide")
    pairs = [(i, i + 1) for i in range(1, n - 1, 2)]
    return lax.ppermute(array, "wide", pairs + [(j, i) for i, j in pairs])


def from_others(array):
    n = lax.axis_size("narrow")
    if n == 2:
        return swap(array, "narrow", 0)
    return jnp.concatenate(
        [lax.ppermute(array, "narrow", [((i + k) % n, i) for i in range(n)]) for k in range(1, n)]
    )


def shards(n_wide, n_narrow, rhs, alpha, beta):
    bx, bz, lanes = rhs.shape
    flat = lambda t: t.reshape(-1, lanes)
    zw = bz * n_narrow
    f32 = jnp.float32
    planes, p1 = bx + 2 * H, bx // 2 + 2 * H1
    n2 = (bx // 4) * (zw // 4)
    vmem, hbm = pl.BlockSpec(memory_space=pltpu.VMEM), pl.BlockSpec(memory_space=pl.ANY)
    keep0 = jax.ShapeDtypeStruct((KEPT, (bx + 4) * zw, lanes), f32)
    keep1 = jax.ShapeDtypeStruct((KEPT, p1 * (zw // 2), lanes), f32)
    u_face = jax.ShapeDtypeStruct((zw, lanes), f32)
    sems = [pltpu.SemaphoreType.DMA((KEPT,)), pltpu.SemaphoreType.DMA((KEPT,))]

    def params(scratch, rows):
        size = 4 * sum(math.prod(t.shape) for t in scratch[:-2]) + 4 * lanes * rows
        return pltpu.CompilerParams(vmem_limit_bytes=min(63 * 2**20, size + size // 8 + 2**21))

    face = jax.ShapeDtypeStruct(((3 * H - 2) * bz, lanes), f32)
    even, odd, own = pl.pallas_call(
        functools.partial(pack_kernel, bx, bz),
        out_shape=[face, face, jax.ShapeDtypeStruct((3 * bx * bz, lanes), f32)],
        in_specs=[hbm] * 3,
        out_specs=[vmem] * 3,
        scratch_shapes=[pltpu.SemaphoreType.DMA((9,))],
        compiler_params=pltpu.CompilerParams(vmem_limit_bytes=2**22),
        name="pack",
    )(flat(rhs), flat(alpha), flat(beta))
    even = swap(even, "wide", 0)
    odd = swap_odd(odd)
    other = from_others(own)
    others = from_others(jnp.concatenate([even, odd]))
    scratch = [
        pltpu.VMEM((9, planes * zw, lanes), f32),
        pltpu.VMEM((9, p1 * (zw // 2), lanes), f32),
        pltpu.VMEM((3, n2, lanes), f32),
        pltpu.VMEM((3, p1 * zw, lanes), f32),
        *sems,
    ]
    packed, ueven, uodd, keep0, keep1 = pl.pallas_call(
        functools.partial(down_kernel, bx, bz, n_wide, n_narrow),
        out_shape=[jax.ShapeDtypeStruct((n2 // n_narrow, lanes), f32), u_face, u_face, keep0, keep1],
        in_specs=[vmem] * 5,
        out_specs=[vmem, vmem, vmem, hbm, hbm],
        scratch_shapes=scratch,
        compiler_params=params(scratch, 3 * planes * zw),
        name="down",
    )(own, even, odd, other, others)
    hodd = swap_odd(uodd)
    gathered = packed
    for bit in reversed(range(bits_of(n_wide))):
        rows = gathered.shape[0]
        sent = jnp.concatenate([gathered, ueven]) if bit == 0 else gathered
        came = swap(sent, "wide", bit)
        gathered = jnp.concatenate([gathered, came[:rows]])
    heven = came[rows:]
    for bit in reversed(range(bits_of(n_narrow))):
        gathered = jnp.concatenate([gathered, swap(gathered, "narrow", bit)])
    nx = n_wide * bx
    scratch = []
    for index in range(2, LEVELS):
        zl = zw // 2**index
        scratch.append(pltpu.VMEM((8, nx // 2**index * zl + 2 * margin(zl, index), lanes), f32))
    scratch += [
        pltpu.VMEM((KEPT + 1, *keep0.shape[1:]), f32),
        pltpu.VMEM((KEPT + 1, (p1 + 2) * (zw // 2), lanes), f32),
        pltpu.VMEM((3, max((bx // 2 + 2) * zw, LONGEST // 2), lanes), f32),
        pltpu.SemaphoreType.DMA,
        *sems,
    ]
    out = pl.pallas_call(
        functools.partial(up_kernel, bx, bz, n_wide, n_narrow),
        out_shape=jax.ShapeDtypeStruct((bx * bz, lanes), f32),
        in_specs=[hbm, vmem, vmem, hbm, hbm],
        out_specs=vmem,
        scratch_shapes=scratch,
        compiler_params=params(scratch[:-3] + sems, bx * bz),
        name="up",
    )(gathered, heven, hodd, keep0, keep1)
    return out.reshape(bx, bz, lanes)


def solution(mesh):
    n_wide, n_narrow = mesh.shape["wide"], mesh.shape["narrow"]
    spec = P("wide", "narrow", None)
    return jax.shard_map(
        functools.partial(shards, n_wide, n_narrow),
        mesh=mesh,
        in_specs=(spec, spec, spec),
        out_specs=spec,
        check_vma=False,
    )
```

```python
import functools
import math

import jax
import jax.numpy as jnp
from jax import lax
from jax.experimental import pallas as pl
from jax.experimental.pallas import tpu as pltpu
from jax.sharding import PartitionSpec as P

LEVELS = 6
BOTTOM = 6
OMEGA = 2.0 / 3.0
LANES = 128
H1 = 3
H = 2 * H1 + 1
LONGEST = 2048


def short(n, rows):
    return n * rows <= LONGEST


def each(n, rows, body):
    if short(n, rows):
        for i in range(n):
            body(i)
    else:

        def step(i, _):
            body(i)
            return 0

        lax.fori_loop(0, n, step, 0)


F, W, CX, CZ, CY, U, A, B, V = range(9)
KEPT = 6


class Level:
    def __init__(self, ref, zw, index, base=0):
        self.ref, self.zw, self.base = ref, zw, base
        self.d, self.s = 2**index, 0.25**index

    def at(self, plane):
        return Level.moved(self, self.base + plane * self.zw)

    def moved(self, base):
        other = Level(self.ref, self.zw, 0, base)
        other.d, other.s = self.d, self.s
        return other

    def get(self, q, r, n):
        return self.ref[q, pl.ds(r, n), :]

    def put(self, q, r, value):
        self.ref[q, pl.ds(r, value.shape[0]), :] = value

    def setup(self, first, count, chunk, valid=None):
        zw, d = self.zw, self.d
        n = chunk * zw
        row = lax.broadcasted_iota(jnp.int32, (n, LANES), 0) % zw
        lane = lax.broadcasted_iota(jnp.int32, (n, LANES), 1)
        z0, z1, y0, y1 = row == 0, row == zw - 1, lane < d, lane >= LANES - d
        hs = 0.5 * self.s

        def body(i):
            p = first + i * chunk
            r = self.base + p * zw
            b = self.get(B, r, n)
            bxp = self.get(B, r + zw, n)
            bxm = self.get(B, r - zw, n)
            bzp = jnp.where(z1, 0.0, self.get(B, r + 1, n))
            bzm = jnp.where(z0, 0.0, self.get(B, r - 1, n))
            byp = jnp.where(y1, 0.0, pltpu.roll(b, LANES - d, 1))
            bym = jnp.where(y0, 0.0, pltpu.roll(b, d, 1))
            dg = self.get(A, r, n) + hs * (6.0 * b + bxp + bxm + bzp + bzm + byp + bym)
            w = OMEGA / dg
            if valid is not None:
                w = jnp.where(valid(p), w, 0.0)
            self.put(A, r, dg)
            self.put(W, r, w)
            self.put(U, r, w * self.get(F, r, n))
            self.put(CX, r, hs * (b + bxp))
            self.put(CZ, r, jnp.where(z1, 0.0, hs * (b + bzp)))
            self.put(CY, r, jnp.where(y1, 0.0, hs * (b + byp)))

        assert count % chunk == 0
        each(count // chunk, n, body)

    def first_cx(self, plane):
        r = self.base + plane * self.zw
        n = self.zw
        self.put(CX, r, (0.5 * self.s) * (self.get(B, r, n) + self.get(B, r + n, n)))

    def around(self, q, r, n):
        zw, d = self.zw, self.d
        v = self.get(q, r, n)
        t = self.get(CX, r, n) * self.get(q, r + zw, n)
        t = t + self.get(CX, r - zw, n) * self.get(q, r - zw, n)
        t = t + self.get(CZ, r, n) * self.get(q, r + 1, n)
        t = t + self.get(CZ, r - 1, n) * self.get(q, r - 1, n)
        cy = self.get(CY, r, n)
        t = t + cy * pltpu.roll(v, LANES - d, 1)
        t = t + pltpu.roll(cy * v, d, 1)
        return v, t

    def sweep(self, src, dst, first, count, chunk):
        n = chunk * self.zw

        def body(i):
            r = self.base + (first + i * chunk) * self.zw
            v, t = self.around(src, r, n)
            self.put(dst, r, (1.0 - OMEGA) * v + self.get(W, r, n) * (self.get(F, r, n) + t))

        assert count % chunk == 0
        each(count // chunk, n, body)

    def residual(self, q, r, n):
        v, t = self.around(q, r, n)
        return self.get(F, r, n) + t - self.get(A, r, n) * v


def lane_pairs(t, d):
    s = t + pltpu.roll(t, LANES - d, 1)
    lane = lax.broadcasted_iota(jnp.int32, t.shape, 1)
    return jnp.where((lane // d) % 2 == 0, s, pltpu.roll(s, d, 1))


def restrict_planes(get, fine, first, pairs, coarse, q, plane, tmp, per):
    zw = fine.zw
    half = zw // 2

    def body(i):
        r = fine.base + (first + 2 * i * per) * zw
        t0 = i * per * zw if short(pairs // per, 2 * per * zw) else 0
        for k in range(per):
            v = get(r + 2 * k * zw, 2 * zw)
            tmp[pl.ds(t0 + k * zw, zw), :] = v[:zw] + v[zw:]
        t = tmp[pl.ds(t0, per * half, 2), :] + tmp[pl.ds(t0 + 1, per * half, 2), :]
        coarse.put(q, coarse.base + plane * half + i * per * half, lane_pairs(t, fine.d) * 0.125)

    assert pairs % per == 0
    each(pairs // per, 2 * per * zw, body)


def restrict_small(value, fine, coarse, q, tmp, count):
    zw, zc = fine.zw, coarse.zw
    tmp[pl.ds(0, count * 2 * zw), :] = value
    for z in range(zc):
        t = None
        for dx in range(2):
            for dz in range(2):
                part = tmp[pl.ds(dx * zw + 2 * z + dz, count, 2 * zw), :]
                t = part if t is None else t + part
        t = lane_pairs(t, fine.d) * 0.125
        if zc == 1:
            coarse.put(q, coarse.base, t)
        else:
            coarse.ref[q, pl.ds(coarse.base + z, count, zc), :] = t


def prolong_small(coarse, q, fine, p, tmp, count):
    zw, zc = fine.zw, coarse.zw
    for z in range(zc):
        v = coarse.get(q, coarse.base, count) if zc == 1 else coarse.ref[q, pl.ds(coarse.base + z, count, zc), :]
        for dx in range(2):
            for dz in range(2):
                tmp[pl.ds(dx * zw + 2 * z + dz, count, 2 * zw), :] = v
    n = count * 2 * zw
    fine.put(p, fine.base, fine.get(p, fine.base, n) + tmp[pl.ds(0, n), :])


def prolong_planes(coarse, q, plane, count, fine, src, dst, first, tmp, per=1):
    zw = fine.zw
    half = zw // 2

    def body(i):
        v = coarse.get(q, coarse.base + (plane + i * per) * half, per * half)
        t0 = i * per * zw if short(count // per, 2 * per * zw) else 0
        tmp[pl.ds(t0, per * half, 2), :] = v
        tmp[pl.ds(t0 + 1, per * half, 2), :] = v
        for k in range(per):
            e = tmp[pl.ds(t0 + k * zw, zw), :]
            r = fine.base + (first + 2 * (i * per + k)) * zw
            fine.put(dst, r, fine.get(src, r, zw) + e)
            fine.put(dst, r + zw, fine.get(src, r + zw, zw) + e)

    assert count % per == 0
    each(count // per, 2 * per * zw, body)


def keep(level, q, first, count, dst, k, sem):
    src = level.ref.at[q, pl.ds(first * level.zw, count * level.zw)]
    copy = pltpu.make_async_copy(src, dst.at[k], sem.at[k])
    copy.start()
    return copy


def pack_kernel(bx, bz, rhs, alpha, beta, even, odd, own, sem):
    up = 1 - lax.axis_index("wide") % 2
    waits = []
    at = [0, 0]
    for q, (src, size) in enumerate(((rhs, H - 1), (alpha, H - 1), (beta, H))):
        for k, dst in enumerate((even, odd)):
            upper = up if k == 0 else 1 - up
            start = pl.multiple_of(upper * ((bx - size) * bz), 8)
            copy = pltpu.make_async_copy(
                src.at[pl.ds(start, size * bz)], dst.at[pl.ds(at[k] * bz, size * bz)], sem.at[2 * q + k]
            )
            copy.start()
            waits.append(copy)
            at[k] += size
        copy = pltpu.make_async_copy(src, own.at[pl.ds(q * bx * bz, bx * bz)], sem.at[6 + q])
        copy.start()
        waits.append(copy)
    for copy in waits:
        copy.wait()


def down_kernel(
    bx, bz, n_wide, n_narrow, own, even, odd, other, others, packed, ueven, uodd, keep0, keep1, lev0, lev1, part, tmp, sem0, sem1
):
    zw = bz * n_narrow
    planes = bx + 2 * H
    wide = lax.axis_index("wide")
    narrow = lax.axis_index("narrow")
    up = 1 - wide % 2
    l0 = Level(lev0, zw, 0)
    l1 = Level(lev1, zw // 2, 1)

    def place(q, src, src_plane, count, plane, z):
        def body(i):
            r = pl.multiple_of((plane + i) * zw + z, 8)
            l0.put(q, r, src[pl.ds((src_plane + i) * bz, bz), :])

        each(count, bz, body)

    g = H - 1
    all_h = 2 * g + H
    for index, (q, at, size) in enumerate(((F, 0, g), (A, g, g), (B, 2 * g, H))):
        above, below = H + bx, H - size
        p_even = up * above + (1 - up) * below
        p_odd = (1 - up) * above + up * below
        place(q, own, index * bx, bx, H, narrow * bz)
        place(q, even, at, size, p_even, narrow * bz)
        place(q, odd, at, size, p_odd, narrow * bz)
        for k in range(n_narrow - 1):
            z = (1 - narrow if n_narrow == 2 else lax.rem(narrow + 1 + k, n_narrow)) * bz
            place(q, other, (3 * k + index) * bx, bx, H, z)
            place(q, others, 2 * k * all_h + at, size, p_even, z)
            place(q, others, (2 * k + 1) * all_h + at, size, p_odd, z)
    first0, count0 = H - 2, bx + 4
    p1 = bx // 2 + 2 * H1
    waits = [keep(l0, F, first0, count0, keep0, F, sem0)]

    def valid0(p):
        x = wide * bx - H + p
        return jnp.logical_and(x >= 0, x < n_wide * bx)

    restrict_planes(lambda r, n: l0.get(B, r, n), l0, 1, p1, l1, B, 0, tmp.at[0], 1)
    restrict_planes(lambda r, n: l0.get(A, r, n), l0, 3, p1 - 2, l1, A, 1, tmp.at[1], 1)
    l0.first_cx(0)
    l0.setup(1, planes - 2, 1, valid0)
    waits += [keep(l0, q, first0, count0, keep0, q, sem0) for q in (W, CX, CZ, CY)]
    l0.sweep(U, V, 2, planes - 4, 1)
    waits.append(keep(l0, V, first0, count0, keep0, U, sem0))
    restrict_planes(lambda r, n: l0.residual(V, r, n), l0, 3, p1 - 2, l1, F, 1, tmp.at[2], 1)

    def valid1(p):
        x = wide * (bx // 2) - H1 + p
        return jnp.logical_and(x >= 0, x < n_wide * (bx // 2))

    k2 = bx // 4
    z2 = zw // 4
    n2 = k2 * z2
    l2 = Level(part, z2, 2)
    restrict_planes(lambda r, n: l1.get(A, r, n), l1, H1, k2, l2, 1, 0, tmp.at[1], 1)
    restrict_planes(lambda r, n: l1.get(B, r, n), l1, H1, k2, l2, 2, 0, tmp.at[0], 1)
    l1.first_cx(0)
    l1.put(CZ, 0, jnp.zeros((l1.zw, LANES), jnp.float32))
    l1.setup(1, p1 - 2, 1, valid1)
    l1.sweep(U, V, 2, p1 - 4, 1)
    waits += [keep(l1, q, 0, p1, keep1, q, sem1) for q in (F, W, CX, CZ, CY)]
    waits.append(keep(l1, V, 0, p1, keep1, U, sem1))
    n1 = 2 * l1.zw
    upper, lower = H1 + bx // 2 - 3, H1 + 1
    ueven[...] = l1.get(V, pl.multiple_of((up * upper + (1 - up) * lower) * l1.zw, 8), n1)
    uodd[...] = l1.get(V, pl.multiple_of(((1 - up) * upper + up * lower) * l1.zw, 8), n1)
    restrict_planes(lambda r, n: l1.residual(V, r, n), l1, H1, k2, l2, 0, 0, tmp.at[2], 1)
    which = lax.broadcasted_iota(jnp.int32, (n2, LANES), 1) % 4
    part[0] = jnp.where(which == 0, part[0], jnp.where(which == 1, part[1], part[2]))
    share = n2 // n_narrow
    mine = part[0, pl.ds(pl.multiple_of(narrow * share, 8), share), :]

    def spread(i):
        packed[pl.ds(i * share, share), :] = mine

    each(n_wide * n_narrow, share, spread)
    for copy in waits:
        copy.wait()


def margin(zl, index):
    return max(8, (4 if index == 2 else 2) * zl)


def up_kernel(
    bx, bz, n_wide, n_narrow, gathered, heven, hodd, keep0, keep1, out, lev2, lev3, lev4, lev5, lev0, lev1, near2, near3, tmp, sem0, sem1
):
    wide = lax.axis_index("wide")
    narrow = lax.axis_index("narrow")
    zw = bz * n_narrow
    fetch = []
    z1 = zw // 2
    for kept, lev, done, r in ((keep1, lev1, sem1, z1), (keep0, lev0, sem0, 0)):
        for q in range(KEPT):
            copy = pltpu.make_async_copy(kept.at[q], lev.at[q, pl.ds(r, kept.shape[1])], done.at[q])
            copy.start()
            fetch.append(copy)
    levels = []
    for index, ref in enumerate((lev2, lev3, lev4, lev5), 2):
        zl = zw // 2**index
        m = margin(zl, index)
        level = Level(ref, zl, index, m)
        level.nx = n_wide * bx // 2**index
        levels.append(level)
        zero = jnp.zeros((m, LANES), jnp.float32)
        for q in (F, W, CX, CZ, CY, U, B):
            level.put(q, 0, zero)
            level.put(q, m + level.nx * zl, zero)
    l2, l3, l4, l5 = levels
    planes2 = bx // 4
    n2 = planes2 * l2.zw
    n = n2 // n_narrow
    lane = lax.broadcasted_iota(jnp.int32, (n, LANES), 1) % 4

    def unpack(i):
        p = gathered[pl.ds(i * n, n), :]
        for q, k, first, second in ((F, 0, 1, 2), (A, 1, LANES - 1, 2), (B, 2, 1, LANES - 2)):
            t = jnp.where(lane == k, p, 0.0)
            t = t + pltpu.roll(t, first, 1)
            t = t + pltpu.roll(t, second, 1)
            l2.put(q, l2.base + i * n, t)

    each(n_wide * n_narrow, n, unpack)

    def chunk_of(level):
        return max(1, min(32 // level.zw, level.nx))

    def down(level, coarse, q, get, t):
        if level.zw >= 8:
            restrict_planes(get, level, 0, coarse.nx, coarse, q, 0, t, max(1, 16 // level.zw))
        else:
            restrict_small(get(level.base, level.nx * level.zw), level, coarse, q, t, coarse.nx)

    for level, coarse in ((l2, l3), (l3, l4), (l4, l5)):
        down(level, coarse, A, lambda r, m, level=level: level.get(A, r, m), tmp.at[0])
        down(level, coarse, B, lambda r, m, level=level: level.get(B, r, m), tmp.at[1])
    for level, coarse in ((l2, l3), (l3, l4), (l4, l5)):
        level.setup(0, level.nx, chunk_of(level))
        level.sweep(U, B, 0, level.nx, chunk_of(level))
        down(level, coarse, F, lambda r, m, level=level: level.residual(B, r, m), tmp.at[0])
    l5.setup(0, l5.nx, chunk_of(l5))
    src, dst = U, B
    for _ in range(BOTTOM - 1):
        l5.sweep(src, dst, 0, l5.nx, chunk_of(l5))
        src, dst = dst, src
    coarse = l5
    for level in (l4, l3):
        if level.zw >= 8:
            prolong_planes(coarse, src, 0, coarse.nx, level, B, B, 0, tmp.at[0], max(1, 16 // level.zw))
        else:
            prolong_small(coarse, src, level, B, tmp.at[0], coarse.nx)
        level.sweep(B, U, 0, level.nx, chunk_of(level))
        level.sweep(U, B, 0, level.nx, chunk_of(level))
        coarse, src = level, B
    start = wide * planes2
    w2 = Level(near2, l2.zw, 2)
    w3 = Level(near3, l3.zw, 3)

    def window(src, q, dst, k, first, count):
        n = count * src.zw
        dst.put(k, 0, src.get(q, pl.multiple_of(src.base + first * src.zw, 8), n))

    window(l3, B, w3, 0, start // 2 - 2, planes2 // 2 + 4)
    for q in (F, W, CX, CZ, CY):
        window(l2, q, w2, q, start - 4, planes2 + 8)
    window(l2, B, w2, U, start - 4, planes2 + 8)
    prolong_planes(w3, 0, 0, planes2 // 2 + 4, w2, U, U, 0, tmp.at[1], 2 if l2.zw < 16 else 1)
    w2.sweep(U, KEPT, 1, planes2 + 6, 2)
    w2.sweep(KEPT, U, 2, planes2 + 4, 2)
    for copy in fetch:
        copy.wait()
    l1 = Level(lev1, z1, 1)
    count1 = bx // 2 + 2 * H1 + 2
    up = 1 - wide % 2
    above, below = H1 + bx // 2 + 2, 1
    l1.put(U, pl.multiple_of((up * above + (1 - up) * below) * z1, 8), heven[...])
    l1.put(U, pl.multiple_of(((1 - up) * above + up * below) * z1, 8), hodd[...])
    prolong_planes(w2, U, 2, count1 // 2, l1, U, U, 0, tmp.at[0])
    l1.sweep(U, KEPT, 2, count1 - 4, 1)
    l1.sweep(KEPT, U, 3, count1 - 6, 1)
    l0 = Level(lev0, zw, 0)
    prolong_planes(l1, U, 3, bx // 2 + 2, l0, U, U, 0, tmp.at[1])
    l0.sweep(U, KEPT, 1, bx + 2, 1)
    l0.sweep(KEPT, U, 2, bx, 1)

    def give(i):
        r = pl.multiple_of((2 + i) * zw + narrow * bz, 8)
        out[pl.ds(i * bz, bz), :] = l0.get(U, r, bz)

    each(bx, bz, give)


def swap(array, axis, bit):
    n = lax.axis_size(axis)
    return lax.ppermute(array, axis, [(i, i ^ (1 << bit)) for i in range(n)])


def swap_odd(array):
    n = lax.axis_size("wide")
    pairs = [(i, i + 1) for i in range(1, n - 1, 2)]
    return lax.ppermute(array, "wide", pairs + [(j, i) for i, j in pairs])


def from_others(array):
    n = lax.axis_size("narrow")
    if n == 2:
        return swap(array, "narrow", 0)
    return jnp.concatenate(
        [lax.ppermute(array, "narrow", [((i + k) % n, i) for i in range(n)]) for k in range(1, n)]
    )


def shards(n_wide, n_narrow, rhs, alpha, beta):
    bx, bz, lanes = rhs.shape
    flat = lambda t: t.reshape(-1, lanes)
    zw = bz * n_narrow
    f32 = jnp.float32
    planes, p1 = bx + 2 * H, bx // 2 + 2 * H1
    n2 = (bx // 4) * (zw // 4)
    vmem, hbm = pl.BlockSpec(memory_space=pltpu.VMEM), pl.BlockSpec(memory_space=pl.ANY)
    keep0 = jax.ShapeDtypeStruct((KEPT, (bx + 4) * zw, lanes), f32)
    keep1 = jax.ShapeDtypeStruct((KEPT, p1 * (zw // 2), lanes), f32)
    u_face = jax.ShapeDtypeStruct((zw, lanes), f32)
    sems = [pltpu.SemaphoreType.DMA((KEPT,)), pltpu.SemaphoreType.DMA((KEPT,))]

    def params(scratch, rows):
        size = 4 * sum(math.prod(t.shape) for t in scratch[:-2]) + 4 * lanes * rows
        return pltpu.CompilerParams(vmem_limit_bytes=min(255 * 2**18, size + size // 8 + 2**21))

    face = jax.ShapeDtypeStruct(((3 * H - 2) * bz, lanes), f32)
    even, odd, own = pl.pallas_call(
        functools.partial(pack_kernel, bx, bz),
        out_shape=[face, face, jax.ShapeDtypeStruct((3 * bx * bz, lanes), f32)],
        in_specs=[pl.BlockSpec(memory_space=pltpu.HBM)] * 3,
        out_specs=[vmem] * 3,
        scratch_shapes=[pltpu.SemaphoreType.DMA((9,))],
        compiler_params=pltpu.CompilerParams(vmem_limit_bytes=62 * 2**20),
        name="pack",
    )(flat(rhs), flat(alpha), flat(beta))
    even = swap(even, "wide", 0)
    odd = swap_odd(odd)
    other = from_others(own)
    others = from_others(jnp.concatenate([even, odd]))
    scratch = [
        pltpu.VMEM((9, planes * zw, lanes), f32),
        pltpu.VMEM((9, p1 * (zw // 2), lanes), f32),
        pltpu.VMEM((3, n2, lanes), f32),
        pltpu.VMEM((3, p1 * zw, lanes), f32),
        *sems,
    ]
    packed, ueven, uodd, keep0, keep1 = pl.pallas_call(
        functools.partial(down_kernel, bx, bz, n_wide, n_narrow),
        out_shape=[jax.ShapeDtypeStruct((n_wide * n2, lanes), f32), u_face, u_face, keep0, keep1],
        in_specs=[vmem] * 5,
        out_specs=[vmem, vmem, vmem, hbm, hbm],
        scratch_shapes=scratch,
        compiler_params=params(scratch, 3 * planes * zw),
        name="down",
    )(own, even, odd, other, others)
    heven, hodd = swap(ueven, "wide", 0), swap_odd(uodd)
    gathered = lax.all_to_all(packed, ("wide", "narrow"), 0, 0, tiled=True)
    nx = n_wide * bx
    scratch = []
    for index in range(2, LEVELS):
        zl = zw // 2**index
        scratch.append(pltpu.VMEM((8, nx // 2**index * zl + 2 * margin(zl, index), lanes), f32))
    scratch += [
        pltpu.VMEM((KEPT + 1, *keep0.shape[1:]), f32),
        pltpu.VMEM((KEPT + 1, (p1 + 2) * (zw // 2), lanes), f32),
        pltpu.VMEM((KEPT + 1, (bx // 4 + 8) * (zw // 4), lanes), f32),
        pltpu.VMEM((1, (bx // 8 + 4) * (zw // 8), lanes), f32),
        pltpu.VMEM((2, LONGEST // 2, lanes), f32),
        *sems,
    ]
    out = pl.pallas_call(
        functools.partial(up_kernel, bx, bz, n_wide, n_narrow),
        out_shape=jax.ShapeDtypeStruct((bx * bz, lanes), f32),
        in_specs=[vmem, vmem, vmem, hbm, hbm],
        out_specs=vmem,
        scratch_shapes=scratch,
        compiler_params=params(scratch, bx * bz + n_wide * n2 + 2 * zw),
        name="up",
    )(gathered, heven, hodd, keep0, keep1)
    return out.reshape(bx, bz, lanes)


def solution(mesh):
    n_wide, n_narrow = mesh.shape["wide"], mesh.shape["narrow"]
    spec = P("wide", "narrow", None)
    return jax.shard_map(
        functools.partial(shards, n_wide, n_narrow),
        mesh=mesh,
        in_specs=(spec, spec, spec),
        out_specs=spec,
        check_vma=False,
    )
```

```python
import functools
import math

import jax
import jax.numpy as jnp
from jax import lax
from jax.experimental import pallas as pl
from jax.experimental.pallas import tpu as pltpu
from jax.sharding import PartitionSpec as P

LEVELS = 6
BOTTOM = 6
OMEGA = 2.0 / 3.0
LANES = 128
H1 = 3
H = 2 * H1 + 1
LONGEST = 2048


def short(n, rows):
    return n * rows <= LONGEST


def each(n, rows, body):
    if short(n, rows):
        for i in range(n):
            body(i)
    else:

        def step(i, _):
            body(i)
            return 0

        lax.fori_loop(0, n, step, 0)


F, W, CX, CZ, CY, U, A, B, V = range(9)
KEPT = 6


class Level:
    def __init__(self, ref, zw, index, base=0):
        self.ref, self.zw, self.base = ref, zw, base
        self.d, self.s = 2**index, 0.25**index

    def at(self, plane):
        return Level.moved(self, self.base + plane * self.zw)

    def moved(self, base):
        other = Level(self.ref, self.zw, 0, base)
        other.d, other.s = self.d, self.s
        return other

    def get(self, q, r, n):
        return self.ref[q, pl.ds(r, n), :]

    def put(self, q, r, value):
        self.ref[q, pl.ds(r, value.shape[0]), :] = value

    def setup(self, first, count, chunk, valid=None):
        zw, d = self.zw, self.d
        n = chunk * zw
        row = lax.broadcasted_iota(jnp.int32, (n, LANES), 0) % zw
        lane = lax.broadcasted_iota(jnp.int32, (n, LANES), 1)
        z0, z1, y0, y1 = row == 0, row == zw - 1, lane < d, lane >= LANES - d
        hs = 0.5 * self.s

        def body(i):
            p = first + i * chunk
            r = self.base + p * zw
            b = self.get(B, r, n)
            bxp = self.get(B, r + zw, n)
            bxm = self.get(B, r - zw, n)
            bzp = jnp.where(z1, 0.0, self.get(B, r + 1, n))
            bzm = jnp.where(z0, 0.0, self.get(B, r - 1, n))
            byp = jnp.where(y1, 0.0, pltpu.roll(b, LANES - d, 1))
            bym = jnp.where(y0, 0.0, pltpu.roll(b, d, 1))
            dg = self.get(A, r, n) + hs * (6.0 * b + bxp + bxm + bzp + bzm + byp + bym)
            w = OMEGA / dg
            if valid is not None:
                w = jnp.where(valid(p), w, 0.0)
            self.put(A, r, dg)
            self.put(W, r, w)
            self.put(U, r, w * self.get(F, r, n))
            self.put(CX, r, hs * (b + bxp))
            self.put(CZ, r, jnp.where(z1, 0.0, hs * (b + bzp)))
            self.put(CY, r, jnp.where(y1, 0.0, hs * (b + byp)))

        assert count % chunk == 0
        each(count // chunk, n, body)

    def first_cx(self, plane):
        r = self.base + plane * self.zw
        n = self.zw
        self.put(CX, r, (0.5 * self.s) * (self.get(B, r, n) + self.get(B, r + n, n)))

    def around(self, q, r, n):
        zw, d = self.zw, self.d
        v = self.get(q, r, n)
        t = self.get(CX, r, n) * self.get(q, r + zw, n)
        t = t + self.get(CX, r - zw, n) * self.get(q, r - zw, n)
        t = t + self.get(CZ, r, n) * self.get(q, r + 1, n)
        t = t + self.get(CZ, r - 1, n) * self.get(q, r - 1, n)
        cy = self.get(CY, r, n)
        t = t + cy * pltpu.roll(v, LANES - d, 1)
        t = t + pltpu.roll(cy * v, d, 1)
        return v, t

    def sweep(self, src, dst, first, count, chunk):
        n = chunk * self.zw

        def body(i):
            r = self.base + (first + i * chunk) * self.zw
            v, t = self.around(src, r, n)
            self.put(dst, r, (1.0 - OMEGA) * v + self.get(W, r, n) * (self.get(F, r, n) + t))

        assert count % chunk == 0
        each(count // chunk, n, body)

    def residual(self, q, r, n):
        v, t = self.around(q, r, n)
        return self.get(F, r, n) + t - self.get(A, r, n) * v


def lane_pairs(t, d):
    s = t + pltpu.roll(t, LANES - d, 1)
    lane = lax.broadcasted_iota(jnp.int32, t.shape, 1)
    return jnp.where((lane // d) % 2 == 0, s, pltpu.roll(s, d, 1))


def restrict_planes(get, fine, first, pairs, coarse, q, plane, tmp, per):
    zw = fine.zw
    half = zw // 2

    def body(i):
        r = fine.base + (first + 2 * i * per) * zw
        t0 = i * per * zw if short(pairs // per, 2 * per * zw) else 0
        for k in range(per):
            v = get(r + 2 * k * zw, 2 * zw)
            tmp[pl.ds(t0 + k * zw, zw), :] = v[:zw] + v[zw:]
        t = tmp[pl.ds(t0, per * half, 2), :] + tmp[pl.ds(t0 + 1, per * half, 2), :]
        coarse.put(q, coarse.base + plane * half + i * per * half, lane_pairs(t, fine.d) * 0.125)

    assert pairs % per == 0
    each(pairs // per, 2 * per * zw, body)


def restrict_small(value, fine, coarse, q, tmp, count):
    zw, zc = fine.zw, coarse.zw
    tmp[pl.ds(0, count * 2 * zw), :] = value
    for z in range(zc):
        t = None
        for dx in range(2):
            for dz in range(2):
                part = tmp[pl.ds(dx * zw + 2 * z + dz, count, 2 * zw), :]
                t = part if t is None else t + part
        t = lane_pairs(t, fine.d) * 0.125
        if zc == 1:
            coarse.put(q, coarse.base, t)
        else:
            coarse.ref[q, pl.ds(coarse.base + z, count, zc), :] = t


def prolong_small(coarse, q, fine, p, tmp, count):
    zw, zc = fine.zw, coarse.zw
    for z in range(zc):
        v = coarse.get(q, coarse.base, count) if zc == 1 else coarse.ref[q, pl.ds(coarse.base + z, count, zc), :]
        for dx in range(2):
            for dz in range(2):
                tmp[pl.ds(dx * zw + 2 * z + dz, count, 2 * zw), :] = v
    n = count * 2 * zw
    fine.put(p, fine.base, fine.get(p, fine.base, n) + tmp[pl.ds(0, n), :])


def prolong_planes(coarse, q, plane, count, fine, src, dst, first, tmp, per=1):
    zw = fine.zw
    half = zw // 2

    def body(i):
        v = coarse.get(q, coarse.base + (plane + i * per) * half, per * half)
        t0 = i * per * zw if short(count // per, 2 * per * zw) else 0
        tmp[pl.ds(t0, per * half, 2), :] = v
        tmp[pl.ds(t0 + 1, per * half, 2), :] = v
        for k in range(per):
            e = tmp[pl.ds(t0 + k * zw, zw), :]
            r = fine.base + (first + 2 * (i * per + k)) * zw
            fine.put(dst, r, fine.get(src, r, zw) + e)
            fine.put(dst, r + zw, fine.get(src, r + zw, zw) + e)

    assert count % per == 0
    each(count // per, 2 * per * zw, body)


def keep(level, q, first, count, dst, k, sem):
    src = level.ref.at[q, pl.ds(first * level.zw, count * level.zw)]
    copy = pltpu.make_async_copy(src, dst.at[k], sem.at[k])
    copy.start()
    return copy


def pack_kernel(bx, bz, rhs, alpha, beta, even, odd, sem):
    up = 1 - lax.axis_index("wide") % 2
    waits = []
    at = 0
    for q, (src, size) in enumerate(((rhs, H - 1), (alpha, H - 1), (beta, H))):
        for k, dst in enumerate((even, odd)):
            upper = up if k == 0 else 1 - up
            start = pl.multiple_of(upper * ((bx - size) * bz), 8)
            copy = pltpu.make_async_copy(
                src.at[pl.ds(start, size * bz)], dst.at[pl.ds(at * bz, size * bz)], sem.at[2 * q + k]
            )
            copy.start()
            waits.append(copy)
        at += size
    for copy in waits:
        copy.wait()


def z_of(narrow, k, n_narrow):
    return 1 - narrow if n_narrow == 2 else lax.rem(narrow + 1 + k, n_narrow)


def spread4(p, lane, k):
    t = jnp.where(lane == k, p, 0.0)
    t = t + pltpu.roll(t, 1 if k % 2 == 0 else LANES - 1, 1)
    return t + pltpu.roll(t, 2 if k < 2 else LANES - 2, 1)


def coarsen_kernel(bx, bz, n_wide, n_narrow, alpha, beta, other_a, other_b, packed, fine, mid, part, tmp):
    zw = bz * n_narrow
    narrow = lax.axis_index("narrow")
    z2 = zw // 4
    for q, own, other in ((0, alpha, other_a), (1, beta, other_b)):

        def place(i, q=q, own=own, other=other):
            fine[q, pl.ds(pl.multiple_of(i * zw + narrow * bz, 8), bz), :] = own[pl.ds(i * bz, bz), :]
            for k in range(n_narrow - 1):
                r = pl.multiple_of(i * zw + z_of(narrow, k, n_narrow) * bz, 8)
                fine[q, pl.ds(r, bz), :] = other[pl.ds((k * bx + i) * bz, bz), :]

        each(bx, zw, place)
    l0, l1, l2 = Level(fine, zw, 0), Level(mid, zw // 2, 1), Level(part, z2, 2)
    for q in range(2):
        restrict_planes(lambda r, n, q=q: l0.get(q, r, n), l0, 0, bx // 2, l1, q, 0, tmp.at[q], 1)
        restrict_planes(lambda r, n, q=q: l1.get(q, r, n), l1, 0, bx // 4, l2, q, 0, tmp.at[q], 1)
    lane = lax.broadcasted_iota(jnp.int32, (z2, LANES), 1) % 4
    for k in range(bx // 8):
        a0, a1 = l2.get(0, 2 * k * z2, z2), l2.get(0, (2 * k + 1) * z2, z2)
        b0, b1 = l2.get(1, 2 * k * z2, z2), l2.get(1, (2 * k + 1) * z2, z2)
        l2.put(2, k * z2, jnp.where(lane == 0, a0, jnp.where(lane == 1, b0, jnp.where(lane == 2, a1, b1))))
    mine = part[2, pl.ds(pl.multiple_of(narrow * 8, 8), 8), :]

    def spread(i):
        packed[pl.ds(i * 8, 8), :] = mine

    each(n_wide * n_narrow, 8, spread)


def down_kernel(
    bx, bz, n_wide, n_narrow, rhs, alpha, beta, even, odd, other_r, other_a, other_b, others, packed, keep0, keep1, lev0, lev1,
    part, tmp, sem0, sem1
):
    zw = bz * n_narrow
    planes = bx + 2 * H
    wide = lax.axis_index("wide")
    narrow = lax.axis_index("narrow")
    up = 1 - wide % 2
    l0 = Level(lev0, zw, 0)
    l1 = Level(lev1, zw // 2, 1)

    def place(q, src, src_plane, count, plane, z):
        def body(i):
            r = pl.multiple_of((plane + i) * zw + z, 8)
            l0.put(q, r, src[pl.ds((src_plane + i) * bz, bz), :])

        each(count, bz, body)

    g = H - 1
    all_h = 2 * g + H
    for q, at, size, own, other in ((F, 0, g, rhs, other_r), (A, g, g, alpha, other_a), (B, 2 * g, H, beta, other_b)):
        above, below = H + bx, H - size
        p_even = up * above + (1 - up) * below
        p_odd = (1 - up) * above + up * below
        place(q, own, 0, bx, H, narrow * bz)
        place(q, even, at, size, p_even, narrow * bz)
        place(q, odd, at, size, p_odd, narrow * bz)
        for k in range(n_narrow - 1):
            z = z_of(narrow, k, n_narrow) * bz
            place(q, other, k * bx, bx, H, z)
            place(q, others, 2 * k * all_h + at, size, p_even, z)
            place(q, others, (2 * k + 1) * all_h + at, size, p_odd, z)
    first0, count0 = H - 2, bx + 4
    p1 = bx // 2 + 2 * H1
    waits = [keep(l0, F, first0, count0, keep0, F, sem0)]

    def valid0(p):
        x = wide * bx - H + p
        return jnp.logical_and(x >= 0, x < n_wide * bx)

    restrict_planes(lambda r, n: l0.get(B, r, n), l0, 1, p1, l1, B, 0, tmp.at[0], 1)
    restrict_planes(lambda r, n: l0.get(A, r, n), l0, 3, p1 - 2, l1, A, 1, tmp.at[1], 1)
    l0.first_cx(0)
    l0.setup(1, planes - 2, 1, valid0)
    waits += [keep(l0, q, first0, count0, keep0, q, sem0) for q in (W, CX, CZ, CY)]
    l0.sweep(U, V, 2, planes - 4, 1)
    waits.append(keep(l0, V, first0, count0, keep0, U, sem0))
    restrict_planes(lambda r, n: l0.residual(V, r, n), l0, 3, p1 - 2, l1, F, 1, tmp.at[2], 1)

    def valid1(p):
        x = wide * (bx // 2) - H1 + p
        return jnp.logical_and(x >= 0, x < n_wide * (bx // 2))

    k2 = bx // 4
    z2 = zw // 4
    n2 = k2 * z2
    l2 = Level(part, z2, 2)
    l1.first_cx(0)
    l1.put(CZ, 0, jnp.zeros((l1.zw, LANES), jnp.float32))
    l1.setup(1, p1 - 2, 1, valid1)
    l1.sweep(U, V, 2, p1 - 4, 1)
    waits += [keep(l1, q, 0, p1, keep1, q, sem1) for q in (F, W, CX, CZ, CY)]
    waits.append(keep(l1, V, 0, p1, keep1, U, sem1))
    restrict_planes(lambda r, n: l1.residual(V, r, n), l1, H1, k2, l2, 0, 0, tmp.at[2], 1)
    which = lax.broadcasted_iota(jnp.int32, (z2, LANES), 1) % 4
    f2 = [part[0, pl.ds(k * z2, z2), :] for k in range(4)]
    part[1, pl.ds(0, z2), :] = jnp.where(
        which == 0, f2[0], jnp.where(which == 1, f2[1], jnp.where(which == 2, f2[2], f2[3]))
    )
    mine = part[1, pl.ds(pl.multiple_of(narrow // 2 * 8, 8), 8), :]
    first = jnp.broadcast_to(lax.broadcasted_iota(jnp.int32, (8, LANES), 1) % 2 == 0, (8, LANES))

    def face(plane):
        r = pl.multiple_of((H1 + plane) * l1.zw + narrow * 8, 8)
        return jnp.where(first, l1.get(V, r, 8), l1.get(V, pl.multiple_of(r + l1.zw, 8), 8))

    upper, lower = face(bx // 2 - 3), face(1)

    def spread(i):
        packed[pl.ds(i * 16, 8), :] = mine
        packed[pl.ds(i * 16 + 8, 8), :] = upper

    each(n_wide * n_narrow, 16, spread)

    @pl.when(wide > 0)
    def _():
        for c in range(n_narrow):
            packed[pl.ds(pl.multiple_of(((wide - 1) * n_narrow + c) * 16 + 8, 8), 8), :] = lower

    for copy in waits:
        copy.wait()


def big(devices):
    return devices > 64


def margin(zl, index):
    return max(8, (4 if index == 2 else 2) * zl)


def up_kernel(
    bx, bz, n_wide, n_narrow, gathered, coarse, keep0, keep1, out, lev2, lev3, lev4, lev5, lev0, lev1, near2, near3, faces, tmp, sem0, sem1
):
    wide = lax.axis_index("wide")
    narrow = lax.axis_index("narrow")
    zw = bz * n_narrow
    fetch = []
    z1 = zw // 2
    for kept, lev, done, r in ((keep1, lev1, sem1, z1), (keep0, lev0, sem0, 0)):
        for q in range(KEPT):
            copy = pltpu.make_async_copy(kept.at[q], lev.at[q, pl.ds(r, kept.shape[1])], done.at[q])
            copy.start()
            fetch.append(copy)
    levels = []
    for index, ref in enumerate((lev2, lev3, lev4, lev5), 2):
        zl = zw // 2**index
        m = margin(zl, index)
        level = Level(ref, zl, index, m)
        level.nx = n_wide * bx // 2**index
        levels.append(level)
        zero = jnp.zeros((m, LANES), jnp.float32)
        for q in (F, W, CX, CZ, CY, U, B):
            level.put(q, 0, zero)
            level.put(q, m + level.nx * zl, zero)
    l2, l3, l4, l5 = levels
    planes2 = bx // 4
    z2 = l2.zw
    devices = n_wide * n_narrow
    if big(devices):
        for src, q in ((gathered, U), (coarse, W)):
            dst = lev2.at[q, pl.ds(l2.base, src.shape[0])]
            pltpu.sync_copy(src, dst)
        read = lambda r: l2.get(U, l2.base + r, 8)
        read_ab = lambda r: l2.get(W, l2.base + r, 8)
    else:
        read = lambda r: gathered[pl.ds(r, 8), :]
        read_ab = lambda r: coarse[pl.ds(r, 8), :]
    lane = lax.broadcasted_iota(jnp.int32, (8, LANES), 1) % 4

    def unpack_ab(i):
        w, c = i // n_narrow, i % n_narrow
        p = read_ab(i * 8)
        pair, z = c * 8 // z2, c * 8 % z2
        r = l2.base + (w * planes2 + 2 * pair) * z2 + z
        for k, (q, plane) in enumerate(((A, 0), (B, 0), (A, 1), (B, 1))):
            l2.put(q, r + plane * z2, spread4(p, lane, k))

    each(devices, 32, unpack_ab)

    def unpack_f(i):
        w, h = i // (n_narrow // 2), i % (n_narrow // 2)
        p = read((w * n_narrow + 2 * h) * 16)
        r = l2.base + w * planes2 * z2 + h * 8
        for k in range(4):
            l2.put(F, r + k * z2, spread4(p, lane, k))

    each(devices // 2, 32, unpack_f)
    even_lane = lane % 2 == 0
    for k, by in ((0, -1), (1, 1)):
        there = wide + by
        valid = jnp.logical_and(there >= 0, there < n_wide)
        there = jnp.clip(there, 0, n_wide - 1)
        for c in range(n_narrow):
            p = jnp.where(valid, read(pl.multiple_of((there * n_narrow + c) * 16 + 8, 8)), 0.0)
            t = jnp.where(even_lane, p, 0.0)
            faces[k, pl.ds(c * 8, 8), :] = t + pltpu.roll(t, 1, 1)
            t = p - t
            faces[k, pl.ds(z1 + c * 8, 8), :] = t + pltpu.roll(t, LANES - 1, 1)

    def chunk_of(level):
        return max(1, min(32 // level.zw, level.nx))

    def down(level, coarse, q, get, t):
        if level.zw >= 8:
            restrict_planes(get, level, 0, coarse.nx, coarse, q, 0, t, max(1, 16 // level.zw))
        else:
            restrict_small(get(level.base, level.nx * level.zw), level, coarse, q, t, coarse.nx)

    for level, coarse in ((l2, l3), (l3, l4), (l4, l5)):
        down(level, coarse, A, lambda r, m, level=level: level.get(A, r, m), tmp.at[0])
        down(level, coarse, B, lambda r, m, level=level: level.get(B, r, m), tmp.at[1])
    for level, coarse in ((l2, l3), (l3, l4), (l4, l5)):
        level.setup(0, level.nx, chunk_of(level))
        level.sweep(U, B, 0, level.nx, chunk_of(level))
        down(level, coarse, F, lambda r, m, level=level: level.residual(B, r, m), tmp.at[0])
    l5.setup(0, l5.nx, chunk_of(l5))
    src, dst = U, B
    for _ in range(BOTTOM - 1):
        l5.sweep(src, dst, 0, l5.nx, chunk_of(l5))
        src, dst = dst, src
    coarse = l5
    for level in (l4, l3):
        if level.zw >= 8:
            prolong_planes(coarse, src, 0, coarse.nx, level, B, B, 0, tmp.at[0], max(1, 16 // level.zw))
        else:
            prolong_small(coarse, src, level, B, tmp.at[0], coarse.nx)
        level.sweep(B, U, 0, level.nx, chunk_of(level))
        level.sweep(U, B, 0, level.nx, chunk_of(level))
        coarse, src = level, B
    start = wide * planes2
    w2 = Level(near2, l2.zw, 2)
    w3 = Level(near3, l3.zw, 3)

    def window(src, q, dst, k, first, count):
        n = count * src.zw
        dst.put(k, 0, src.get(q, pl.multiple_of(src.base + first * src.zw, 8), n))

    window(l3, B, w3, 0, start // 2 - 2, planes2 // 2 + 4)
    for q in (F, W, CX, CZ, CY):
        window(l2, q, w2, q, start - 4, planes2 + 8)
    window(l2, B, w2, U, start - 4, planes2 + 8)
    prolong_planes(w3, 0, 0, planes2 // 2 + 4, w2, U, U, 0, tmp.at[1], 2 if l2.zw < 16 else 1)
    w2.sweep(U, KEPT, 1, planes2 + 6, 2)
    w2.sweep(KEPT, U, 2, planes2 + 4, 2)
    for copy in fetch:
        copy.wait()
    l1 = Level(lev1, z1, 1)
    count1 = bx // 2 + 2 * H1 + 2
    l1.put(U, z1, faces[0])
    l1.put(U, (H1 + bx // 2 + 2) * z1, faces[1])
    prolong_planes(w2, U, 2, count1 // 2, l1, U, U, 0, tmp.at[0])
    l1.sweep(U, KEPT, 2, count1 - 4, 1)
    l1.sweep(KEPT, U, 3, count1 - 6, 1)
    l0 = Level(lev0, zw, 0)
    prolong_planes(l1, U, 3, bx // 2 + 2, l0, U, U, 0, tmp.at[1])
    l0.sweep(U, KEPT, 1, bx + 2, 1)
    l0.sweep(KEPT, U, 2, bx, 1)

    def give(i):
        r = pl.multiple_of((2 + i) * zw + narrow * bz, 8)
        out[pl.ds(i * bz, bz), :] = l0.get(U, r, bz)

    each(bx, bz, give)


def swap(array, axis, bit):
    n = lax.axis_size(axis)
    return lax.ppermute(array, axis, [(i, i ^ (1 << bit)) for i in range(n)])


def swap_odd(array):
    n = lax.axis_size("wide")
    pairs = [(i, i + 1) for i in range(1, n - 1, 2)]
    return lax.ppermute(array, "wide", pairs + [(j, i) for i, j in pairs])


def from_others(array):
    n = lax.axis_size("narrow")
    if n == 2:
        return swap(array, "narrow", 0)
    return jnp.concatenate(
        [lax.ppermute(array, "narrow", [((i + k) % n, i) for i in range(n)]) for k in range(1, n)]
    )


def shards(n_wide, n_narrow, rhs, alpha, beta):
    bx, bz, lanes = rhs.shape
    flat = lambda t: t.reshape(-1, lanes)
    zw = bz * n_narrow
    f32 = jnp.float32
    planes, p1 = bx + 2 * H, bx // 2 + 2 * H1
    n2 = (bx // 4) * (zw // 4)
    vmem, hbm = pl.BlockSpec(memory_space=pltpu.VMEM), pl.BlockSpec(memory_space=pl.ANY)
    keep0 = jax.ShapeDtypeStruct((KEPT, (bx + 4) * zw, lanes), f32)
    keep1 = jax.ShapeDtypeStruct((KEPT, p1 * (zw // 2), lanes), f32)
    sems = [pltpu.SemaphoreType.DMA((KEPT,)), pltpu.SemaphoreType.DMA((KEPT,))]

    def params(scratch, rows):
        size = 4 * sum(math.prod(t.shape) for t in scratch if t.dtype == f32) + 4 * lanes * rows
        return pltpu.CompilerParams(vmem_limit_bytes=min(255 * 2**18, size + size // 8 + 2**21))

    face = jax.ShapeDtypeStruct(((3 * H - 2) * bz, lanes), f32)
    even, odd = pl.pallas_call(
        functools.partial(pack_kernel, bx, bz),
        out_shape=[face, face],
        in_specs=[pl.BlockSpec(memory_space=pltpu.HBM)] * 3,
        out_specs=[hbm] * 2,
        scratch_shapes=[pltpu.SemaphoreType.DMA((6,))],
        compiler_params=pltpu.CompilerParams(vmem_limit_bytes=62 * 2**20),
        name="pack",
    )(flat(rhs), flat(alpha), flat(beta))
    even = swap(even, "wide", 0)
    odd = swap_odd(odd)
    other_b, other_a, other_r = from_others(flat(beta)), from_others(flat(alpha)), from_others(flat(rhs))
    devices = n_wide * n_narrow
    scratch = [
        pltpu.VMEM((2, bx * zw, lanes), f32),
        pltpu.VMEM((2, bx // 2 * (zw // 2), lanes), f32),
        pltpu.VMEM((3, n2, lanes), f32),
        pltpu.VMEM((2, max(bx * zw // 2, LONGEST // 2), lanes), f32),
    ]
    coarse = pl.pallas_call(
        functools.partial(coarsen_kernel, bx, bz, n_wide, n_narrow),
        out_shape=jax.ShapeDtypeStruct((devices * 8, lanes), f32),
        in_specs=[vmem] * 4,
        out_specs=vmem,
        scratch_shapes=scratch,
        compiler_params=params(scratch + [], 2 * bx * zw + devices * 8),
        name="coarsen",
    )(flat(alpha), flat(beta), other_a, other_b)
    coarse = lax.all_to_all(coarse, ("wide", "narrow"), 0, 0, tiled=True)
    even, odd, coarse = lax.optimization_barrier((even, odd, coarse))
    others = from_others(jnp.concatenate([even, odd]))
    scratch = [
        pltpu.VMEM((9, planes * zw, lanes), f32),
        pltpu.VMEM((9, p1 * (zw // 2), lanes), f32),
        pltpu.VMEM((3, n2, lanes), f32),
        pltpu.VMEM((3, p1 * zw, lanes), f32),
        *sems,
    ]
    packed, keep0, keep1 = pl.pallas_call(
        functools.partial(down_kernel, bx, bz, n_wide, n_narrow),
        out_shape=[jax.ShapeDtypeStruct((devices * 16, lanes), f32), keep0, keep1],
        in_specs=[vmem] * 9,
        out_specs=[vmem, hbm, hbm],
        scratch_shapes=scratch,
        compiler_params=params(scratch, 3 * planes * zw),
        name="down",
    )(flat(rhs), flat(alpha), flat(beta), even, odd, other_r, other_a, other_b, others)
    gathered = lax.all_to_all(packed, ("wide", "narrow"), 0, 0, tiled=True)
    nx = n_wide * bx
    scratch = []
    for index in range(2, LEVELS):
        zl = zw // 2**index
        scratch.append(pltpu.VMEM((8, nx // 2**index * zl + 2 * margin(zl, index), lanes), f32))
    scratch += [
        pltpu.VMEM((KEPT + 1, *keep0.shape[1:]), f32),
        pltpu.VMEM((KEPT + 1, (p1 + 2) * (zw // 2), lanes), f32),
        pltpu.VMEM((KEPT + 1, (bx // 4 + 8) * (zw // 4), lanes), f32),
        pltpu.VMEM((1, (bx // 8 + 4) * (zw // 8), lanes), f32),
        pltpu.VMEM((2, zw, lanes), f32),
        pltpu.VMEM((2, LONGEST // 2, lanes), f32),
        *sems,
    ]
    out = pl.pallas_call(
        functools.partial(up_kernel, bx, bz, n_wide, n_narrow),
        out_shape=jax.ShapeDtypeStruct((bx * bz, lanes), f32),
        in_specs=[hbm if big(devices) else vmem] * 2 + [hbm, hbm],
        out_specs=vmem,
        scratch_shapes=scratch,
        compiler_params=params(scratch, bx * bz + devices * 24),
        name="up",
    )(gathered, coarse, keep0, keep1)
    return out.reshape(bx, bz, lanes)


def solution(mesh):
    n_wide, n_narrow = mesh.shape["wide"], mesh.shape["narrow"]
    spec = P("wide", "narrow", None)
    return jax.shard_map(
        functools.partial(shards, n_wide, n_narrow),
        mesh=mesh,
        in_specs=(spec, spec, spec),
        out_specs=spec,
        check_vma=False,
    )
```

```python
import functools
import math

import jax
import jax.numpy as jnp
from jax import lax
from jax.experimental import pallas as pl
from jax.experimental.pallas import tpu as pltpu
from jax.sharding import PartitionSpec as P

LEVELS = 6
BOTTOM = 6
OMEGA = 2.0 / 3.0
LANES = 128
H1 = 3
H = 2 * H1 + 1
LONGEST = 2048


def short(n, rows):
    return n * rows <= LONGEST


def each(n, rows, body):
    if short(n, rows):
        for i in range(n):
            body(i)
    else:

        def step(i, _):
            body(i)
            return 0

        lax.fori_loop(0, n, step, 0)


F, W, CX, CZ, CY, U, A, B, V = range(9)
KEPT = 6


class Level:
    def __init__(self, ref, zw, index, base=0):
        self.ref, self.zw, self.base = ref, zw, base
        self.d, self.s = 2**index, 0.25**index

    def at(self, plane):
        return Level.moved(self, self.base + plane * self.zw)

    def moved(self, base):
        other = Level(self.ref, self.zw, 0, base)
        other.d, other.s = self.d, self.s
        return other

    def get(self, q, r, n):
        return self.ref[q, pl.ds(r, n), :]

    def put(self, q, r, value):
        self.ref[q, pl.ds(r, value.shape[0]), :] = value

    def setup(self, first, count, chunk, valid=None):
        zw, d = self.zw, self.d
        n = chunk * zw
        row = lax.broadcasted_iota(jnp.int32, (n, LANES), 0) % zw
        lane = lax.broadcasted_iota(jnp.int32, (n, LANES), 1)
        z0, z1, y0, y1 = row == 0, row == zw - 1, lane < d, lane >= LANES - d
        hs = 0.5 * self.s

        def body(i):
            p = first + i * chunk
            r = self.base + p * zw
            b = self.get(B, r, n)
            bxp = self.get(B, r + zw, n)
            bxm = self.get(B, r - zw, n)
            bzp = jnp.where(z1, 0.0, self.get(B, r + 1, n))
            bzm = jnp.where(z0, 0.0, self.get(B, r - 1, n))
            byp = jnp.where(y1, 0.0, pltpu.roll(b, LANES - d, 1))
            bym = jnp.where(y0, 0.0, pltpu.roll(b, d, 1))
            dg = self.get(A, r, n) + hs * (6.0 * b + bxp + bxm + bzp + bzm + byp + bym)
            w = OMEGA / dg
            if valid is not None:
                w = jnp.where(valid(p), w, 0.0)
            self.put(A, r, dg)
            self.put(W, r, w)
            self.put(U, r, w * self.get(F, r, n))
            self.put(CX, r, hs * (b + bxp))
            self.put(CZ, r, jnp.where(z1, 0.0, hs * (b + bzp)))
            self.put(CY, r, jnp.where(y1, 0.0, hs * (b + byp)))

        assert count % chunk == 0
        each(count // chunk, n, body)

    def first_cx(self, plane):
        r = self.base + plane * self.zw
        n = self.zw
        self.put(CX, r, (0.5 * self.s) * (self.get(B, r, n) + self.get(B, r + n, n)))

    def around(self, q, r, n):
        zw, d = self.zw, self.d
        v = self.get(q, r, n)
        t = self.get(CX, r, n) * self.get(q, r + zw, n)
        t = t + self.get(CX, r - zw, n) * self.get(q, r - zw, n)
        t = t + self.get(CZ, r, n) * self.get(q, r + 1, n)
        t = t + self.get(CZ, r - 1, n) * self.get(q, r - 1, n)
        cy = self.get(CY, r, n)
        t = t + cy * pltpu.roll(v, LANES - d, 1)
        t = t + pltpu.roll(cy * v, d, 1)
        return v, t

    def sweep(self, src, dst, first, count, chunk):
        n = chunk * self.zw

        def body(i):
            r = self.base + (first + i * chunk) * self.zw
            v, t = self.around(src, r, n)
            self.put(dst, r, (1.0 - OMEGA) * v + self.get(W, r, n) * (self.get(F, r, n) + t))

        assert count % chunk == 0
        each(count // chunk, n, body)

    def residual(self, q, r, n):
        v, t = self.around(q, r, n)
        return self.get(F, r, n) + t - self.get(A, r, n) * v


def lane_pairs(t, d):
    s = t + pltpu.roll(t, LANES - d, 1)
    lane = lax.broadcasted_iota(jnp.int32, t.shape, 1)
    return jnp.where((lane // d) % 2 == 0, s, pltpu.roll(s, d, 1))


def restrict_planes(get, fine, first, pairs, coarse, q, plane, tmp, per):
    zw = fine.zw
    half = zw // 2

    def body(i):
        r = fine.base + (first + 2 * i * per) * zw
        t0 = i * per * zw if short(pairs // per, 2 * per * zw) else 0
        for k in range(per):
            v = get(r + 2 * k * zw, 2 * zw)
            tmp[pl.ds(t0 + k * zw, zw), :] = v[:zw] + v[zw:]
        t = tmp[pl.ds(t0, per * half, 2), :] + tmp[pl.ds(t0 + 1, per * half, 2), :]
        coarse.put(q, coarse.base + plane * half + i * per * half, lane_pairs(t, fine.d) * 0.125)

    assert pairs % per == 0
    each(pairs // per, 2 * per * zw, body)


def restrict_small(value, fine, coarse, q, tmp, count):
    zw, zc = fine.zw, coarse.zw
    tmp[pl.ds(0, count * 2 * zw), :] = value
    for z in range(zc):
        t = None
        for dx in range(2):
            for dz in range(2):
                part = tmp[pl.ds(dx * zw + 2 * z + dz, count, 2 * zw), :]
                t = part if t is None else t + part
        t = lane_pairs(t, fine.d) * 0.125
        if zc == 1:
            coarse.put(q, coarse.base, t)
        else:
            coarse.ref[q, pl.ds(coarse.base + z, count, zc), :] = t


def prolong_small(coarse, q, fine, p, tmp, count):
    zw, zc = fine.zw, coarse.zw
    for z in range(zc):
        v = coarse.get(q, coarse.base, count) if zc == 1 else coarse.ref[q, pl.ds(coarse.base + z, count, zc), :]
        for dx in range(2):
            for dz in range(2):
                tmp[pl.ds(dx * zw + 2 * z + dz, count, 2 * zw), :] = v
    n = count * 2 * zw
    fine.put(p, fine.base, fine.get(p, fine.base, n) + tmp[pl.ds(0, n), :])


def prolong_planes(coarse, q, plane, count, fine, src, dst, first, tmp, per=1):
    zw = fine.zw
    half = zw // 2

    def body(i):
        v = coarse.get(q, coarse.base + (plane + i * per) * half, per * half)
        t0 = i * per * zw if short(count // per, 2 * per * zw) else 0
        tmp[pl.ds(t0, per * half, 2), :] = v
        tmp[pl.ds(t0 + 1, per * half, 2), :] = v
        for k in range(per):
            e = tmp[pl.ds(t0 + k * zw, zw), :]
            r = fine.base + (first + 2 * (i * per + k)) * zw
            fine.put(dst, r, fine.get(src, r, zw) + e)
            fine.put(dst, r + zw, fine.get(src, r + zw, zw) + e)

    assert count % per == 0
    each(count // per, 2 * per * zw, body)


def keep(level, q, first, count, dst, k, sem):
    src = level.ref.at[q, pl.ds(first * level.zw, count * level.zw)]
    copy = pltpu.make_async_copy(src, dst.at[k], sem.at[k])
    copy.start()
    return copy


def pack_kernel(bx, bz, rhs, alpha, beta, even, odd, sem):
    up = 1 - lax.axis_index("wide") % 2
    waits = []
    at = 0
    for q, (src, size) in enumerate(((rhs, H - 1), (alpha, H - 1), (beta, H))):
        for k, dst in enumerate((even, odd)):
            upper = up if k == 0 else 1 - up
            start = pl.multiple_of(upper * ((bx - size) * bz), 8)
            copy = pltpu.make_async_copy(
                src.at[pl.ds(start, size * bz)], dst.at[pl.ds(at * bz, size * bz)], sem.at[2 * q + k]
            )
            copy.start()
            waits.append(copy)
        at += size
    for copy in waits:
        copy.wait()


def z_of(narrow, k, n_narrow):
    return 1 - narrow if n_narrow == 2 else lax.rem(narrow + 1 + k, n_narrow)


def spread4(p, lane, k):
    t = jnp.where(lane == k, p, 0.0)
    t = t + pltpu.roll(t, 1 if k % 2 == 0 else LANES - 1, 1)
    return t + pltpu.roll(t, 2 if k < 2 else LANES - 2, 1)


def down_kernel(
    bx, bz, n_wide, n_narrow, own, even, odd, other, others, packed, keep0, keep1, lev0, lev1, part, tmp, sem0, sem1
):
    zw = bz * n_narrow
    planes = bx + 2 * H
    wide = lax.axis_index("wide")
    narrow = lax.axis_index("narrow")
    up = 1 - wide % 2
    l0 = Level(lev0, zw, 0)
    l1 = Level(lev1, zw // 2, 1)

    def place(q, src, src_plane, count, plane, z):
        def body(i):
            r = pl.multiple_of((plane + i) * zw + z, 8)
            l0.put(q, r, src[pl.ds((src_plane + i) * bz, bz), :])

        each(count, bz, body)

    g = H - 1
    all_h = 2 * g + H
    for index, (q, at, size) in enumerate(((F, 0, g), (A, g, g), (B, 2 * g, H))):
        above, below = H + bx, H - size
        p_even = up * above + (1 - up) * below
        p_odd = (1 - up) * above + up * below
        place(q, own, index * bx, bx, H, narrow * bz)
        place(q, even, at, size, p_even, narrow * bz)
        place(q, odd, at, size, p_odd, narrow * bz)
        for k in range(n_narrow - 1):
            z = z_of(narrow, k, n_narrow) * bz
            place(q, other, (3 * k + index) * bx, bx, H, z)
            place(q, others, 2 * k * all_h + at, size, p_even, z)
            place(q, others, (2 * k + 1) * all_h + at, size, p_odd, z)
    first0, count0 = H - 2, bx + 4
    p1 = bx // 2 + 2 * H1
    waits = [keep(l0, F, first0, count0, keep0, F, sem0)]

    def valid0(p):
        x = wide * bx - H + p
        return jnp.logical_and(x >= 0, x < n_wide * bx)

    restrict_planes(lambda r, n: l0.get(B, r, n), l0, 1, p1, l1, B, 0, tmp.at[0], 1)
    restrict_planes(lambda r, n: l0.get(A, r, n), l0, 3, p1 - 2, l1, A, 1, tmp.at[1], 1)
    l0.first_cx(0)
    l0.setup(1, planes - 2, 1, valid0)
    waits += [keep(l0, q, first0, count0, keep0, q, sem0) for q in (W, CX, CZ, CY)]
    l0.sweep(U, V, 2, planes - 4, 1)
    waits.append(keep(l0, V, first0, count0, keep0, U, sem0))
    restrict_planes(lambda r, n: l0.residual(V, r, n), l0, 3, p1 - 2, l1, F, 1, tmp.at[2], 1)

    def valid1(p):
        x = wide * (bx // 2) - H1 + p
        return jnp.logical_and(x >= 0, x < n_wide * (bx // 2))

    k2 = bx // 4
    z2 = zw // 4
    n2 = k2 * z2
    l2 = Level(part, z2, 2)
    restrict_planes(lambda r, n: l1.get(A, r, n), l1, H1, k2, l2, 1, 0, tmp.at[1], 1)
    restrict_planes(lambda r, n: l1.get(B, r, n), l1, H1, k2, l2, 2, 0, tmp.at[0], 1)
    l1.first_cx(0)
    l1.put(CZ, 0, jnp.zeros((l1.zw, LANES), jnp.float32))
    l1.setup(1, p1 - 2, 1, valid1)
    l1.sweep(U, V, 2, p1 - 4, 1)
    waits += [keep(l1, q, 0, p1, keep1, q, sem1) for q in (F, W, CX, CZ, CY)]
    waits.append(keep(l1, V, 0, p1, keep1, U, sem1))
    restrict_planes(lambda r, n: l1.residual(V, r, n), l1, H1, k2, l2, 0, 0, tmp.at[2], 1)
    which = lax.broadcasted_iota(jnp.int32, (z2, LANES), 1) % 4
    fs, as_, bs = [[part[q, pl.ds(k * z2, z2), :] for k in range(4)] for q in range(3)]

    def four(p):
        return jnp.where(which == 0, p[0], jnp.where(which == 1, p[1], jnp.where(which == 2, p[2], p[3])))

    parts = [four(fs), four((as_[0], bs[0], as_[1], bs[1])), four((as_[2], bs[2], as_[3], bs[3]))]
    z1 = l1.zw
    first = lax.broadcasted_iota(jnp.int32, (z1, LANES), 1) % 2 == 0

    def face(plane):
        r = (H1 + plane) * z1
        return jnp.where(first, l1.get(V, r, z1), l1.get(V, r + z1, z1))

    upper, lower = face(bx // 2 - 3), face(1)
    slot = 3 * z2 + z1

    def spread(i):
        for k in range(3):
            packed[pl.ds(i * slot + k * z2, z2), :] = parts[k]
        packed[pl.ds(i * slot + 3 * z2, z1), :] = upper

    each(n_wide, slot, spread)

    @pl.when(wide > 0)
    def _():
        packed[pl.ds(pl.multiple_of((wide - 1) * slot + 3 * z2, 8), z1), :] = lower

    for copy in waits:
        copy.wait()


def big(n_wide):
    return n_wide > 32


def margin(zl, index):
    return max(8, (4 if index == 2 else 2) * zl)


def up_kernel(
    bx, bz, n_wide, n_narrow, gathered, keep0, keep1, out, lev2, lev3, lev4, lev5, lev0, lev1, near2, near3, faces, slots, tmp, sem0, sem1
):
    wide = lax.axis_index("wide")
    narrow = lax.axis_index("narrow")
    zw = bz * n_narrow
    fetch = []
    z1 = zw // 2
    for kept, lev, done, r in ((keep1, lev1, sem1, z1), (keep0, lev0, sem0, 0)):
        for q in range(KEPT):
            copy = pltpu.make_async_copy(kept.at[q], lev.at[q, pl.ds(r, kept.shape[1])], done.at[q])
            copy.start()
            fetch.append(copy)
    levels = []
    for index, ref in enumerate((lev2, lev3, lev4, lev5), 2):
        zl = zw // 2**index
        m = margin(zl, index)
        level = Level(ref, zl, index, m)
        level.nx = n_wide * bx // 2**index
        levels.append(level)
        zero = jnp.zeros((m, LANES), jnp.float32)
        for q in (F, W, CX, CZ, CY, U, B):
            level.put(q, 0, zero)
            level.put(q, m + level.nx * zl, zero)
    l2, l3, l4, l5 = levels
    planes2 = bx // 4
    z2 = l2.zw
    slot = 3 * z2 + z1
    lane = lax.broadcasted_iota(jnp.int32, (z2, LANES), 1) % 4

    def slot_of(w):
        if not big(n_wide):
            return gathered, w * slot
        pltpu.sync_copy(gathered.at[pl.ds(pl.multiple_of(w * slot, 8), slot)], slots)
        return slots, 0

    def unpack(w):
        src, at = slot_of(w)
        r = l2.base + w * planes2 * z2
        for part, wanted in (
            (0, ((F, 0), (F, 1), (F, 2), (F, 3))),
            (1, ((A, 0), (B, 0), (A, 1), (B, 1))),
            (2, ((A, 2), (B, 2), (A, 3), (B, 3))),
        ):
            p = src[pl.ds(at + part * z2, z2), :]
            for k, (q, plane) in enumerate(wanted):
                l2.put(q, r + plane * z2, spread4(p, lane, k))

    each(n_wide, 12 * z2, unpack)
    first = lax.broadcasted_iota(jnp.int32, (z1, LANES), 1) % 2 == 0
    for k, by in ((0, -1), (1, 1)):
        there = wide + by
        valid = jnp.logical_and(there >= 0, there < n_wide)
        src, at = slot_of(jnp.clip(there, 0, n_wide - 1))
        p = jnp.where(valid, src[pl.ds(pl.multiple_of(at + 3 * z2, 8), z1), :], 0.0)
        t = jnp.where(first, p, 0.0)
        faces[k, pl.ds(0, z1), :] = t + pltpu.roll(t, 1, 1)
        t = p - t
        faces[k, pl.ds(z1, z1), :] = t + pltpu.roll(t, LANES - 1, 1)

    def chunk_of(level):
        return max(1, min(32 // level.zw, level.nx))

    def down(level, coarse, q, get, t):
        if level.zw >= 8:
            restrict_planes(get, level, 0, coarse.nx, coarse, q, 0, t, max(1, 16 // level.zw))
        else:
            restrict_small(get(level.base, level.nx * level.zw), level, coarse, q, t, coarse.nx)

    for level, coarse in ((l2, l3), (l3, l4), (l4, l5)):
        down(level, coarse, A, lambda r, m, level=level: level.get(A, r, m), tmp.at[0])
        down(level, coarse, B, lambda r, m, level=level: level.get(B, r, m), tmp.at[1])
    for level, coarse in ((l2, l3), (l3, l4), (l4, l5)):
        level.setup(0, level.nx, chunk_of(level))
        level.sweep(U, B, 0, level.nx, chunk_of(level))
        down(level, coarse, F, lambda r, m, level=level: level.residual(B, r, m), tmp.at[0])
    l5.setup(0, l5.nx, chunk_of(l5))
    src, dst = U, B
    for _ in range(BOTTOM - 1):
        l5.sweep(src, dst, 0, l5.nx, chunk_of(l5))
        src, dst = dst, src
    coarse = l5
    for level in (l4, l3):
        if level.zw >= 8:
            prolong_planes(coarse, src, 0, coarse.nx, level, B, B, 0, tmp.at[0], max(1, 16 // level.zw))
        else:
            prolong_small(coarse, src, level, B, tmp.at[0], coarse.nx)
        level.sweep(B, U, 0, level.nx, chunk_of(level))
        level.sweep(U, B, 0, level.nx, chunk_of(level))
        coarse, src = level, B
    start = wide * planes2
    w2 = Level(near2, l2.zw, 2)
    w3 = Level(near3, l3.zw, 3)

    def window(src, q, dst, k, first, count):
        n = count * src.zw
        dst.put(k, 0, src.get(q, pl.multiple_of(src.base + first * src.zw, 8), n))

    window(l3, B, w3, 0, start // 2 - 2, planes2 // 2 + 4)
    for q in (F, W, CX, CZ, CY):
        window(l2, q, w2, q, start - 4, planes2 + 8)
    window(l2, B, w2, U, start - 4, planes2 + 8)
    prolong_planes(w3, 0, 0, planes2 // 2 + 4, w2, U, U, 0, tmp.at[1], 2 if l2.zw < 16 else 1)
    w2.sweep(U, KEPT, 1, planes2 + 6, 2)
    w2.sweep(KEPT, U, 2, planes2 + 4, 2)
    for copy in fetch:
        copy.wait()
    l1 = Level(lev1, z1, 1)
    count1 = bx // 2 + 2 * H1 + 2
    l1.put(U, z1, faces[0])
    l1.put(U, (H1 + bx // 2 + 2) * z1, faces[1])
    prolong_planes(w2, U, 2, count1 // 2, l1, U, U, 0, tmp.at[0])
    l1.sweep(U, KEPT, 2, count1 - 4, 1)
    l1.sweep(KEPT, U, 3, count1 - 6, 1)
    l0 = Level(lev0, zw, 0)
    prolong_planes(l1, U, 3, bx // 2 + 2, l0, U, U, 0, tmp.at[1])
    l0.sweep(U, KEPT, 1, bx + 2, 1)
    l0.sweep(KEPT, U, 2, bx, 1)

    def give(i):
        r = pl.multiple_of((2 + i) * zw + narrow * bz, 8)
        out[pl.ds(i * bz, bz), :] = l0.get(U, r, bz)

    each(bx, bz, give)


def swap(array, axis, bit):
    n = lax.axis_size(axis)
    return lax.ppermute(array, axis, [(i, i ^ (1 << bit)) for i in range(n)])


def swap_odd(array):
    n = lax.axis_size("wide")
    pairs = [(i, i + 1) for i in range(1, n - 1, 2)]
    return lax.ppermute(array, "wide", pairs + [(j, i) for i, j in pairs])


def from_others(array):
    n = lax.axis_size("narrow")
    if n == 2:
        return swap(array, "narrow", 0)
    return jnp.concatenate(
        [lax.ppermute(array, "narrow", [((i + k) % n, i) for i in range(n)]) for k in range(1, n)]
    )


def shards(n_wide, n_narrow, rhs, alpha, beta):
    bx, bz, lanes = rhs.shape
    flat = lambda t: t.reshape(-1, lanes)
    zw = bz * n_narrow
    f32 = jnp.float32
    planes, p1 = bx + 2 * H, bx // 2 + 2 * H1
    n2 = (bx // 4) * (zw // 4)
    vmem, hbm = pl.BlockSpec(memory_space=pltpu.VMEM), pl.BlockSpec(memory_space=pl.ANY)
    keep0 = jax.ShapeDtypeStruct((KEPT, (bx + 4) * zw, lanes), f32)
    keep1 = jax.ShapeDtypeStruct((KEPT, p1 * (zw // 2), lanes), f32)
    sems = [pltpu.SemaphoreType.DMA((KEPT,)), pltpu.SemaphoreType.DMA((KEPT,))]

    def params(scratch, rows):
        size = 4 * sum(math.prod(t.shape) for t in scratch if t.dtype == f32) + 4 * lanes * rows
        return pltpu.CompilerParams(vmem_limit_bytes=min(255 * 2**18, size + size // 8 + 2**21))

    face = jax.ShapeDtypeStruct(((3 * H - 2) * bz, lanes), f32)
    even, odd = pl.pallas_call(
        functools.partial(pack_kernel, bx, bz),
        out_shape=[face, face],
        in_specs=[pl.BlockSpec(memory_space=pltpu.HBM)] * 3,
        out_specs=[hbm] * 2,
        scratch_shapes=[pltpu.SemaphoreType.DMA((6,))],
        compiler_params=pltpu.CompilerParams(vmem_limit_bytes=62 * 2**20),
        name="pack",
    )(flat(rhs), flat(alpha), flat(beta))
    even, odd, rhs, alpha, beta = lax.optimization_barrier((even, odd, rhs, alpha, beta))
    own = jnp.concatenate([flat(rhs), flat(alpha), flat(beta)])
    even = swap(even, "wide", 0)
    odd = swap_odd(odd)
    other = from_others(own)
    others = from_others(jnp.concatenate([even, odd]))
    slot = 3 * (zw // 4) + zw // 2
    scratch = [
        pltpu.VMEM((9, planes * zw, lanes), f32),
        pltpu.VMEM((9, p1 * (zw // 2), lanes), f32),
        pltpu.VMEM((3, n2, lanes), f32),
        pltpu.VMEM((3, p1 * zw, lanes), f32),
        *sems,
    ]
    packed, keep0, keep1 = pl.pallas_call(
        functools.partial(down_kernel, bx, bz, n_wide, n_narrow),
        out_shape=[jax.ShapeDtypeStruct((n_wide * slot, lanes), f32), keep0, keep1],
        in_specs=[vmem] * 5,
        out_specs=[vmem, hbm, hbm],
        scratch_shapes=scratch,
        compiler_params=params(scratch, 3 * planes * zw),
        name="down",
    )(own, even, odd, other, others)
    gathered = lax.all_to_all(packed, "wide", 0, 0, tiled=True)
    nx = n_wide * bx
    scratch = []
    for index in range(2, LEVELS):
        zl = zw // 2**index
        scratch.append(pltpu.VMEM((8, nx // 2**index * zl + 2 * margin(zl, index), lanes), f32))
    scratch += [
        pltpu.VMEM((KEPT + 1, *keep0.shape[1:]), f32),
        pltpu.VMEM((KEPT + 1, (p1 + 2) * (zw // 2), lanes), f32),
        pltpu.VMEM((KEPT + 1, (bx // 4 + 8) * (zw // 4), lanes), f32),
        pltpu.VMEM((1, (bx // 8 + 4) * (zw // 8), lanes), f32),
        pltpu.VMEM((2, zw, lanes), f32),
        pltpu.VMEM((slot, lanes), f32),
        pltpu.VMEM((2, LONGEST // 2, lanes), f32),
        *sems,
    ]
    out = pl.pallas_call(
        functools.partial(up_kernel, bx, bz, n_wide, n_narrow),
        out_shape=jax.ShapeDtypeStruct((bx * bz, lanes), f32),
        in_specs=[hbm if big(n_wide) else vmem, hbm, hbm],
        out_specs=vmem,
        scratch_shapes=scratch,
        compiler_params=params(scratch, bx * bz + (0 if big(n_wide) else n_wide * slot)),
        name="up",
    )(gathered, keep0, keep1)
    return out.reshape(bx, bz, lanes)


def solution(mesh):
    n_wide, n_narrow = mesh.shape["wide"], mesh.shape["narrow"]
    spec = P("wide", "narrow", None)
    return jax.shard_map(
        functools.partial(shards, n_wide, n_narrow),
        mesh=mesh,
        in_specs=(spec, spec, spec),
        out_specs=spec,
        check_vma=False,
    )
```

```python
import functools
import math

import jax
import jax.numpy as jnp
from jax import lax
from jax.experimental import pallas as pl
from jax.experimental.pallas import tpu as pltpu
from jax.sharding import PartitionSpec as P

LEVELS = 6
BOTTOM = 6
OMEGA = 2.0 / 3.0
LANES = 128
H1 = 3
H = 2 * H1 + 1
LONGEST = 2048


def short(n, rows):
    return n * rows <= LONGEST


def each(n, rows, body):
    if short(n, rows):
        for i in range(n):
            body(i)
    else:

        def step(i, _):
            body(i)
            return 0

        lax.fori_loop(0, n, step, 0)


F, W, CX, CZ, CY, U, A, B, V = range(9)
KEPT = 6


class Level:
    def __init__(self, ref, zw, index, base=0):
        self.ref, self.zw, self.base = ref, zw, base
        self.d, self.s = 2**index, 0.25**index

    def at(self, plane):
        return Level.moved(self, self.base + plane * self.zw)

    def moved(self, base):
        other = Level(self.ref, self.zw, 0, base)
        other.d, other.s = self.d, self.s
        return other

    def get(self, q, r, n):
        return self.ref[q, pl.ds(r, n), :]

    def put(self, q, r, value):
        self.ref[q, pl.ds(r, value.shape[0]), :] = value

    def setup(self, first, count, chunk, valid=None):
        zw, d = self.zw, self.d
        n = chunk * zw
        row = lax.broadcasted_iota(jnp.int32, (n, LANES), 0) % zw
        lane = lax.broadcasted_iota(jnp.int32, (n, LANES), 1)
        z0, z1, y0, y1 = row == 0, row == zw - 1, lane < d, lane >= LANES - d
        hs = 0.5 * self.s

        def body(i):
            p = first + i * chunk
            r = self.base + p * zw
            b = self.get(B, r, n)
            bxp = self.get(B, r + zw, n)
            bxm = self.get(B, r - zw, n)
            bzp = jnp.where(z1, 0.0, self.get(B, r + 1, n))
            bzm = jnp.where(z0, 0.0, self.get(B, r - 1, n))
            byp = jnp.where(y1, 0.0, pltpu.roll(b, LANES - d, 1))
            bym = jnp.where(y0, 0.0, pltpu.roll(b, d, 1))
            dg = self.get(A, r, n) + hs * (6.0 * b + bxp + bxm + bzp + bzm + byp + bym)
            w = OMEGA / dg
            if valid is not None:
                w = jnp.where(valid(p), w, 0.0)
            self.put(A, r, dg)
            self.put(W, r, w)
            self.put(U, r, w * self.get(F, r, n))
            self.put(CX, r, hs * (b + bxp))
            self.put(CZ, r, jnp.where(z1, 0.0, hs * (b + bzp)))
            self.put(CY, r, jnp.where(y1, 0.0, hs * (b + byp)))

        assert count % chunk == 0
        each(count // chunk, n, body)

    def first_cx(self, plane):
        r = self.base + plane * self.zw
        n = self.zw
        self.put(CX, r, (0.5 * self.s) * (self.get(B, r, n) + self.get(B, r + n, n)))

    def around(self, q, r, n):
        zw, d = self.zw, self.d
        v = self.get(q, r, n)
        t = self.get(CX, r, n) * self.get(q, r + zw, n)
        t = t + self.get(CX, r - zw, n) * self.get(q, r - zw, n)
        t = t + self.get(CZ, r, n) * self.get(q, r + 1, n)
        t = t + self.get(CZ, r - 1, n) * self.get(q, r - 1, n)
        cy = self.get(CY, r, n)
        t = t + cy * pltpu.roll(v, LANES - d, 1)
        t = t + pltpu.roll(cy * v, d, 1)
        return v, t

    def sweep(self, src, dst, first, count, chunk):
        n = chunk * self.zw

        def body(i):
            r = self.base + (first + i * chunk) * self.zw
            v, t = self.around(src, r, n)
            self.put(dst, r, (1.0 - OMEGA) * v + self.get(W, r, n) * (self.get(F, r, n) + t))

        assert count % chunk == 0
        each(count // chunk, n, body)

    def residual(self, q, r, n):
        v, t = self.around(q, r, n)
        return self.get(F, r, n) + t - self.get(A, r, n) * v


def lane_pairs(t, d):
    s = t + pltpu.roll(t, LANES - d, 1)
    lane = lax.broadcasted_iota(jnp.int32, t.shape, 1)
    return jnp.where((lane // d) % 2 == 0, s, pltpu.roll(s, d, 1))


def restrict_planes(get, fine, first, pairs, coarse, q, plane, tmp, per):
    zw = fine.zw
    half = zw // 2

    def body(i):
        r = fine.base + (first + 2 * i * per) * zw
        t0 = i * per * zw if short(pairs // per, 2 * per * zw) else 0
        for k in range(per):
            v = get(r + 2 * k * zw, 2 * zw)
            tmp[pl.ds(t0 + k * zw, zw), :] = v[:zw] + v[zw:]
        t = tmp[pl.ds(t0, per * half, 2), :] + tmp[pl.ds(t0 + 1, per * half, 2), :]
        coarse.put(q, coarse.base + plane * half + i * per * half, lane_pairs(t, fine.d) * 0.125)

    assert pairs % per == 0
    each(pairs // per, 2 * per * zw, body)


def restrict_small(value, fine, coarse, q, tmp, count):
    zw, zc = fine.zw, coarse.zw
    tmp[pl.ds(0, count * 2 * zw), :] = value
    for z in range(zc):
        t = None
        for dx in range(2):
            for dz in range(2):
                part = tmp[pl.ds(dx * zw + 2 * z + dz, count, 2 * zw), :]
                t = part if t is None else t + part
        t = lane_pairs(t, fine.d) * 0.125
        if zc == 1:
            coarse.put(q, coarse.base, t)
        else:
            coarse.ref[q, pl.ds(coarse.base + z, count, zc), :] = t


def prolong_small(coarse, q, fine, p, tmp, count):
    zw, zc = fine.zw, coarse.zw
    for z in range(zc):
        v = coarse.get(q, coarse.base, count) if zc == 1 else coarse.ref[q, pl.ds(coarse.base + z, count, zc), :]
        for dx in range(2):
            for dz in range(2):
                tmp[pl.ds(dx * zw + 2 * z + dz, count, 2 * zw), :] = v
    n = count * 2 * zw
    fine.put(p, fine.base, fine.get(p, fine.base, n) + tmp[pl.ds(0, n), :])


def prolong_planes(coarse, q, plane, count, fine, src, dst, first, tmp, per=1):
    zw = fine.zw
    half = zw // 2

    def body(i):
        v = coarse.get(q, coarse.base + (plane + i * per) * half, per * half)
        t0 = i * per * zw if short(count // per, 2 * per * zw) else 0
        tmp[pl.ds(t0, per * half, 2), :] = v
        tmp[pl.ds(t0 + 1, per * half, 2), :] = v
        for k in range(per):
            e = tmp[pl.ds(t0 + k * zw, zw), :]
            r = fine.base + (first + 2 * (i * per + k)) * zw
            fine.put(dst, r, fine.get(src, r, zw) + e)
            fine.put(dst, r + zw, fine.get(src, r + zw, zw) + e)

    assert count % per == 0
    each(count // per, 2 * per * zw, body)


def keep(level, q, first, count, dst, k, sem):
    src = level.ref.at[q, pl.ds(first * level.zw, count * level.zw)]
    copy = pltpu.make_async_copy(src, dst.at[k], sem.at[k])
    copy.start()
    return copy


def pack_kernel(bx, bz, rhs, alpha, beta, even, odd, sem):
    up = 1 - lax.axis_index("wide") % 2
    waits = []
    at = 0
    for q, (src, size) in enumerate(((rhs, H - 1), (alpha, H - 1), (beta, H))):
        for k, dst in enumerate((even, odd)):
            upper = up if k == 0 else 1 - up
            start = pl.multiple_of(upper * ((bx - size) * bz), 8)
            copy = pltpu.make_async_copy(
                src.at[pl.ds(start, size * bz)], dst.at[pl.ds(at * bz, size * bz)], sem.at[2 * q + k]
            )
            copy.start()
            waits.append(copy)
        at += size
    for copy in waits:
        copy.wait()


def z_of(narrow, k, n_narrow):
    return 1 - narrow if n_narrow == 2 else lax.rem(narrow + 1 + k, n_narrow)


def spread4(p, lane, k):
    t = jnp.where(lane == k, p, 0.0)
    t = t + pltpu.roll(t, 1 if k % 2 == 0 else LANES - 1, 1)
    return t + pltpu.roll(t, 2 if k < 2 else LANES - 2, 1)


def coarsen_kernel(bx, bz, devices, alpha, beta, packed, fine, mid, part, tmp, sem):
    z2 = bz // 4
    waits = [pltpu.make_async_copy(src, fine.at[q], sem.at[q]) for q, src in enumerate((alpha, beta))]
    for copy in waits:
        copy.start()
    for copy in waits:
        copy.wait()
    l0, l1, l2 = Level(fine, bz, 0), Level(mid, bz // 2, 1), Level(part, z2, 2)
    for q in range(2):
        restrict_planes(lambda r, n, q=q: l0.get(q, r, n), l0, 0, bx // 2, l1, q, 0, tmp.at[q], 1)
        restrict_planes(lambda r, n, q=q: l1.get(q, r, n), l1, 0, bx // 4, l2, q, 0, tmp.at[q], 2)
    lane = lax.broadcasted_iota(jnp.int32, (z2, LANES), 1) % 4
    for k in range(bx // 8):
        a0, a1 = l2.get(0, 2 * k * z2, z2), l2.get(0, (2 * k + 1) * z2, z2)
        b0, b1 = l2.get(1, 2 * k * z2, z2), l2.get(1, (2 * k + 1) * z2, z2)
        l2.put(2, k * z2, jnp.where(lane == 0, a0, jnp.where(lane == 1, b0, jnp.where(lane == 2, a1, b1))))
    n = bx // 8 * z2
    mine = part[2, pl.ds(0, n), :]

    def spread(i):
        packed[pl.ds(i * n, n), :] = mine

    each(devices, n, spread)


def down_kernel(
    bx, bz, n_wide, n_narrow, own, even, odd, other, others, packed, keep0, keep1, lev0, lev1, part, tmp, sem0, sem1
):
    zw = bz * n_narrow
    planes = bx + 2 * H
    wide = lax.axis_index("wide")
    narrow = lax.axis_index("narrow")
    up = 1 - wide % 2
    l0 = Level(lev0, zw, 0)
    l1 = Level(lev1, zw // 2, 1)

    def place(q, src, src_plane, count, plane, z):
        def body(i):
            r = pl.multiple_of((plane + i) * zw + z, 8)
            l0.put(q, r, src[pl.ds((src_plane + i) * bz, bz), :])

        each(count, bz, body)

    g = H - 1
    all_h = 2 * g + H
    for index, (q, at, size) in enumerate(((F, 0, g), (A, g, g), (B, 2 * g, H))):
        above, below = H + bx, H - size
        p_even = up * above + (1 - up) * below
        p_odd = (1 - up) * above + up * below
        place(q, own, index * bx, bx, H, narrow * bz)
        place(q, even, at, size, p_even, narrow * bz)
        place(q, odd, at, size, p_odd, narrow * bz)
        for k in range(n_narrow - 1):
            z = z_of(narrow, k, n_narrow) * bz
            place(q, other, (3 * k + index) * bx, bx, H, z)
            place(q, others, 2 * k * all_h + at, size, p_even, z)
            place(q, others, (2 * k + 1) * all_h + at, size, p_odd, z)
    first0, count0 = H - 2, bx + 4
    p1 = bx // 2 + 2 * H1
    waits = [keep(l0, F, first0, count0, keep0, F, sem0)]

    def valid0(p):
        x = wide * bx - H + p
        return jnp.logical_and(x >= 0, x < n_wide * bx)

    restrict_planes(lambda r, n: l0.get(B, r, n), l0, 1, p1, l1, B, 0, tmp.at[0], 1)
    restrict_planes(lambda r, n: l0.get(A, r, n), l0, 3, p1 - 2, l1, A, 1, tmp.at[1], 1)
    l0.first_cx(0)
    l0.setup(1, planes - 2, 1, valid0)
    waits += [keep(l0, q, first0, count0, keep0, q, sem0) for q in (W, CX, CZ, CY)]
    l0.sweep(U, V, 2, planes - 4, 1)
    waits.append(keep(l0, V, first0, count0, keep0, U, sem0))
    restrict_planes(lambda r, n: l0.residual(V, r, n), l0, 3, p1 - 2, l1, F, 1, tmp.at[2], 1)

    def valid1(p):
        x = wide * (bx // 2) - H1 + p
        return jnp.logical_and(x >= 0, x < n_wide * (bx // 2))

    k2 = bx // 4
    z2 = zw // 4
    n2 = k2 * z2
    l2 = Level(part, z2, 2)
    l1.first_cx(0)
    l1.put(CZ, 0, jnp.zeros((l1.zw, LANES), jnp.float32))
    l1.setup(1, p1 - 2, 1, valid1)
    l1.sweep(U, V, 2, p1 - 4, 1)
    waits += [keep(l1, q, 0, p1, keep1, q, sem1) for q in (F, W, CX, CZ, CY)]
    waits.append(keep(l1, V, 0, p1, keep1, U, sem1))
    restrict_planes(lambda r, n: l1.residual(V, r, n), l1, H1, k2, l2, 0, 0, tmp.at[2], 1)
    which = lax.broadcasted_iota(jnp.int32, (z2, LANES), 1) % 4
    p = [part[0, pl.ds(k * z2, z2), :] for k in range(4)]
    mine = jnp.where(which == 0, p[0], jnp.where(which == 1, p[1], jnp.where(which == 2, p[2], p[3])))
    z1 = l1.zw
    first = lax.broadcasted_iota(jnp.int32, (z1, LANES), 1) % 2 == 0

    def face(plane):
        r = (H1 + plane) * z1
        return jnp.where(first, l1.get(V, r, z1), l1.get(V, r + z1, z1))

    upper, lower = face(bx // 2 - 3), face(1)
    slot = z2 + z1

    def spread(i):
        packed[pl.ds(i * slot, z2), :] = mine
        packed[pl.ds(i * slot + z2, z1), :] = upper

    each(n_wide, slot, spread)

    @pl.when(wide > 0)
    def _():
        packed[pl.ds(pl.multiple_of((wide - 1) * slot + z2, 8), z1), :] = lower

    for copy in waits:
        copy.wait()


def big(n_wide):
    return n_wide > 32


def margin(zl, index):
    return max(8, (4 if index == 2 else 2) * zl)


def up_kernel(
    bx, bz, n_wide, n_narrow, gathered, coarse, keep0, keep1, out, lev2, lev3, lev4, lev5, lev0, lev1, near2, near3, faces, slots, tmp, sem0, sem1
):
    wide = lax.axis_index("wide")
    narrow = lax.axis_index("narrow")
    zw = bz * n_narrow
    fetch = []
    z1 = zw // 2
    for kept, lev, done, r in ((keep1, lev1, sem1, z1), (keep0, lev0, sem0, 0)):
        for q in range(KEPT):
            copy = pltpu.make_async_copy(kept.at[q], lev.at[q, pl.ds(r, kept.shape[1])], done.at[q])
            copy.start()
            fetch.append(copy)
    levels = []
    for index, ref in enumerate((lev2, lev3, lev4, lev5), 2):
        zl = zw // 2**index
        m = margin(zl, index)
        level = Level(ref, zl, index, m)
        level.nx = n_wide * bx // 2**index
        levels.append(level)
        zero = jnp.zeros((m, LANES), jnp.float32)
        for q in (F, W, CX, CZ, CY, U, B):
            level.put(q, 0, zero)
            level.put(q, m + level.nx * zl, zero)
    l2, l3, l4, l5 = levels
    planes2 = bx // 4
    z2 = l2.zw
    slot = z2 + z1
    lane = lax.broadcasted_iota(jnp.int32, (z2, LANES), 1) % 4

    def slot_of(w):
        if not big(n_wide):
            return gathered, w * slot
        pltpu.sync_copy(gathered.at[pl.ds(pl.multiple_of(w * slot, 8), slot)], slots)
        return slots, 0

    zs = bz // 4
    n = planes2 // 2 * zs
    lane_ab = lax.broadcasted_iota(jnp.int32, (n, LANES), 1) % 4

    def unpack_ab(i):
        w, c = i // n_narrow, i % n_narrow
        if big(n_wide):
            pltpu.sync_copy(coarse.at[pl.ds(pl.multiple_of(i * n, 8), n)], slots.at[pl.ds(0, n)])
            p = slots[pl.ds(0, n), :]
        else:
            p = coarse[pl.ds(i * n, n), :]
        r = l2.base + w * planes2 * z2 + c * zs
        for k, (q, plane) in enumerate(((A, 0), (B, 0), (A, 1), (B, 1))):
            t = spread4(p, lane_ab, k)
            for pair in range(planes2 // 2):
                l2.put(q, r + (2 * pair + plane) * z2, t[pair * zs : (pair + 1) * zs])

    each(n_wide * n_narrow, 32, unpack_ab)

    def unpack(w):
        src, at = slot_of(w)
        r = l2.base + w * planes2 * z2
        p = src[pl.ds(at, z2), :]
        for k in range(4):
            l2.put(F, r + k * z2, spread4(p, lane, k))

    each(n_wide, 4 * z2, unpack)
    first = lax.broadcasted_iota(jnp.int32, (z1, LANES), 1) % 2 == 0
    for k, by in ((0, -1), (1, 1)):
        there = wide + by
        valid = jnp.logical_and(there >= 0, there < n_wide)
        src, at = slot_of(jnp.clip(there, 0, n_wide - 1))
        p = jnp.where(valid, src[pl.ds(pl.multiple_of(at + z2, 8), z1), :], 0.0)
        t = jnp.where(first, p, 0.0)
        faces[k, pl.ds(0, z1), :] = t + pltpu.roll(t, 1, 1)
        t = p - t
        faces[k, pl.ds(z1, z1), :] = t + pltpu.roll(t, LANES - 1, 1)

    def chunk_of(level):
        return max(1, min(32 // level.zw, level.nx))

    def down(level, coarse, q, get, t):
        if level.zw >= 8:
            restrict_planes(get, level, 0, coarse.nx, coarse, q, 0, t, max(1, 16 // level.zw))
        else:
            restrict_small(get(level.base, level.nx * level.zw), level, coarse, q, t, coarse.nx)

    for level, coarse in ((l2, l3), (l3, l4), (l4, l5)):
        down(level, coarse, A, lambda r, m, level=level: level.get(A, r, m), tmp.at[0])
        down(level, coarse, B, lambda r, m, level=level: level.get(B, r, m), tmp.at[1])
    for level, coarse in ((l2, l3), (l3, l4), (l4, l5)):
        level.setup(0, level.nx, chunk_of(level))
        level.sweep(U, B, 0, level.nx, chunk_of(level))
        down(level, coarse, F, lambda r, m, level=level: level.residual(B, r, m), tmp.at[0])
    l5.setup(0, l5.nx, chunk_of(l5))
    src, dst = U, B
    for _ in range(BOTTOM - 1):
        l5.sweep(src, dst, 0, l5.nx, chunk_of(l5))
        src, dst = dst, src
    coarse = l5
    for level in (l4, l3):
        if level.zw >= 8:
            prolong_planes(coarse, src, 0, coarse.nx, level, B, B, 0, tmp.at[0], max(1, 16 // level.zw))
        else:
            prolong_small(coarse, src, level, B, tmp.at[0], coarse.nx)
        level.sweep(B, U, 0, level.nx, chunk_of(level))
        level.sweep(U, B, 0, level.nx, chunk_of(level))
        coarse, src = level, B
    start = wide * planes2
    w2 = Level(near2, l2.zw, 2)
    w3 = Level(near3, l3.zw, 3)

    def window(src, q, dst, k, first, count):
        n = count * src.zw
        dst.put(k, 0, src.get(q, pl.multiple_of(src.base + first * src.zw, 8), n))

    window(l3, B, w3, 0, start // 2 - 2, planes2 // 2 + 4)
    for q in (F, W, CX, CZ, CY):
        window(l2, q, w2, q, start - 4, planes2 + 8)
    window(l2, B, w2, U, start - 4, planes2 + 8)
    prolong_planes(w3, 0, 0, planes2 // 2 + 4, w2, U, U, 0, tmp.at[1], 2 if l2.zw < 16 else 1)
    w2.sweep(U, KEPT, 1, planes2 + 6, 2)
    w2.sweep(KEPT, U, 2, planes2 + 4, 2)
    for copy in fetch:
        copy.wait()
    l1 = Level(lev1, z1, 1)
    count1 = bx // 2 + 2 * H1 + 2
    l1.put(U, z1, faces[0])
    l1.put(U, (H1 + bx // 2 + 2) * z1, faces[1])
    prolong_planes(w2, U, 2, count1 // 2, l1, U, U, 0, tmp.at[0])
    l1.sweep(U, KEPT, 2, count1 - 4, 1)
    l1.sweep(KEPT, U, 3, count1 - 6, 1)
    l0 = Level(lev0, zw, 0)
    prolong_planes(l1, U, 3, bx // 2 + 2, l0, U, U, 0, tmp.at[1])
    l0.sweep(U, KEPT, 1, bx + 2, 1)
    l0.sweep(KEPT, U, 2, bx, 1)

    def give(i):
        r = pl.multiple_of((2 + i) * zw + narrow * bz, 8)
        out[pl.ds(i * bz, bz), :] = l0.get(U, r, bz)

    each(bx, bz, give)


def swap(array, axis, bit):
    n = lax.axis_size(axis)
    return lax.ppermute(array, axis, [(i, i ^ (1 << bit)) for i in range(n)])


def swap_odd(array):
    n = lax.axis_size("wide")
    pairs = [(i, i + 1) for i in range(1, n - 1, 2)]
    return lax.ppermute(array, "wide", pairs + [(j, i) for i, j in pairs])


def from_others(array):
    n = lax.axis_size("narrow")
    if n == 2:
        return swap(array, "narrow", 0)
    return jnp.concatenate(
        [lax.ppermute(array, "narrow", [((i + k) % n, i) for i in range(n)]) for k in range(1, n)]
    )


def shards(n_wide, n_narrow, rhs, alpha, beta):
    bx, bz, lanes = rhs.shape
    flat = lambda t: t.reshape(-1, lanes)
    zw = bz * n_narrow
    f32 = jnp.float32
    planes, p1 = bx + 2 * H, bx // 2 + 2 * H1
    n2 = (bx // 4) * (zw // 4)
    vmem, hbm = pl.BlockSpec(memory_space=pltpu.VMEM), pl.BlockSpec(memory_space=pl.ANY)
    keep0 = jax.ShapeDtypeStruct((KEPT, (bx + 4) * zw, lanes), f32)
    keep1 = jax.ShapeDtypeStruct((KEPT, p1 * (zw // 2), lanes), f32)
    sems = [pltpu.SemaphoreType.DMA((KEPT,)), pltpu.SemaphoreType.DMA((KEPT,))]

    def params(scratch, rows):
        size = 4 * sum(math.prod(t.shape) for t in scratch if t.dtype == f32) + 4 * lanes * rows
        return pltpu.CompilerParams(vmem_limit_bytes=min(255 * 2**18, size + size // 8 + 2**21))

    face = jax.ShapeDtypeStruct(((3 * H - 2) * bz, lanes), f32)
    even, odd = pl.pallas_call(
        functools.partial(pack_kernel, bx, bz),
        out_shape=[face, face],
        in_specs=[pl.BlockSpec(memory_space=pltpu.HBM)] * 3,
        out_specs=[vmem] * 2,
        scratch_shapes=[pltpu.SemaphoreType.DMA((6,))],
        compiler_params=pltpu.CompilerParams(vmem_limit_bytes=62 * 2**20),
        name="pack",
    )(flat(rhs), flat(alpha), flat(beta))
    even, odd, rhs, alpha, beta = lax.optimization_barrier((even, odd, rhs, alpha, beta))
    devices = n_wide * n_narrow
    n8 = bx // 8 * (bz // 4)
    coarse = pl.pallas_call(
        functools.partial(coarsen_kernel, bx, bz, devices),
        out_shape=jax.ShapeDtypeStruct((devices * n8, lanes), f32),
        in_specs=[pl.BlockSpec(memory_space=pltpu.HBM)] * 2,
        out_specs=vmem,
        scratch_shapes=[
            pltpu.VMEM((2, bx * bz, lanes), f32),
            pltpu.VMEM((2, bx * bz // 4, lanes), f32),
            pltpu.VMEM((3, bx * bz // 16, lanes), f32),
            pltpu.VMEM((2, bx * bz // 2, lanes), f32),
            pltpu.SemaphoreType.DMA((2,)),
        ],
        compiler_params=pltpu.CompilerParams(vmem_limit_bytes=62 * 2**20),
        name="coarsen",
    )(flat(alpha), flat(beta))
    coarse = lax.all_to_all(coarse, ("wide", "narrow"), 0, 0, tiled=True)
    own = jnp.concatenate([flat(rhs), flat(alpha), flat(beta)])
    even = swap(even, "wide", 0)
    odd = swap_odd(odd)
    other = from_others(own)
    even, odd, coarse = lax.optimization_barrier((even, odd, coarse))
    others = from_others(jnp.concatenate([even, odd]))
    slot = zw // 4 + zw // 2
    scratch = [
        pltpu.VMEM((9, planes * zw, lanes), f32),
        pltpu.VMEM((9, p1 * (zw // 2), lanes), f32),
        pltpu.VMEM((3, n2, lanes), f32),
        pltpu.VMEM((3, p1 * zw, lanes), f32),
        *sems,
    ]
    packed, keep0, keep1 = pl.pallas_call(
        functools.partial(down_kernel, bx, bz, n_wide, n_narrow),
        out_shape=[jax.ShapeDtypeStruct((n_wide * slot, lanes), f32), keep0, keep1],
        in_specs=[vmem] * 5,
        out_specs=[vmem, hbm, hbm],
        scratch_shapes=scratch,
        compiler_params=params(scratch, 3 * planes * zw),
        name="down",
    )(own, even, odd, other, others)
    gathered = lax.all_to_all(packed, "wide", 0, 0, tiled=True)
    nx = n_wide * bx
    scratch = []
    for index in range(2, LEVELS):
        zl = zw // 2**index
        scratch.append(pltpu.VMEM((8, nx // 2**index * zl + 2 * margin(zl, index), lanes), f32))
    scratch += [
        pltpu.VMEM((KEPT + 1, *keep0.shape[1:]), f32),
        pltpu.VMEM((KEPT + 1, (p1 + 2) * (zw // 2), lanes), f32),
        pltpu.VMEM((KEPT + 1, (bx // 4 + 8) * (zw // 4), lanes), f32),
        pltpu.VMEM((1, (bx // 8 + 4) * (zw // 8), lanes), f32),
        pltpu.VMEM((2, zw, lanes), f32),
        pltpu.VMEM((slot, lanes), f32),
        pltpu.VMEM((2, LONGEST // 2, lanes), f32),
        *sems,
    ]
    out = pl.pallas_call(
        functools.partial(up_kernel, bx, bz, n_wide, n_narrow),
        out_shape=jax.ShapeDtypeStruct((bx * bz, lanes), f32),
        in_specs=[hbm if big(n_wide) else vmem] * 2 + [hbm, hbm],
        out_specs=vmem,
        scratch_shapes=scratch,
        compiler_params=params(scratch, bx * bz + (0 if big(n_wide) else n_wide * slot + devices * n8)),
        name="up",
    )(gathered, coarse, keep0, keep1)
    return out.reshape(bx, bz, lanes)


def solution(mesh):
    n_wide, n_narrow = mesh.shape["wide"], mesh.shape["narrow"]
    spec = P("wide", "narrow", None)
    return jax.shard_map(
        functools.partial(shards, n_wide, n_narrow),
        mesh=mesh,
        in_specs=(spec, spec, spec),
        out_specs=spec,
        check_vma=False,
    )
```

```python
import functools
import math

import jax
import jax.numpy as jnp
from jax import lax
from jax.experimental import pallas as pl
from jax.experimental.pallas import tpu as pltpu
from jax.sharding import PartitionSpec as P

LEVELS = 6
BOTTOM = 6
OMEGA = 2.0 / 3.0
LANES = 128
H1 = 3
H = 2 * H1 + 1
LONGEST = 2048


def short(n, rows):
    return n * rows <= LONGEST


def each(n, rows, body):
    if short(n, rows):
        for i in range(n):
            body(i)
    else:

        def step(i, _):
            body(i)
            return 0

        lax.fori_loop(0, n, step, 0)


F, W, CX, CZ, CY, U, A, B, V = range(9)
KEPT = 6


class Level:
    def __init__(self, ref, zw, index, base=0):
        self.ref, self.zw, self.base = ref, zw, base
        self.d, self.s = 2**index, 0.25**index

    def at(self, plane):
        return Level.moved(self, self.base + plane * self.zw)

    def moved(self, base):
        other = Level(self.ref, self.zw, 0, base)
        other.d, other.s = self.d, self.s
        return other

    def get(self, q, r, n):
        return self.ref[q, pl.ds(r, n), :]

    def put(self, q, r, value):
        self.ref[q, pl.ds(r, value.shape[0]), :] = value

    def setup(self, first, count, chunk, valid=None):
        zw, d = self.zw, self.d
        n = chunk * zw
        row = lax.broadcasted_iota(jnp.int32, (n, LANES), 0) % zw
        lane = lax.broadcasted_iota(jnp.int32, (n, LANES), 1)
        z0, z1, y0, y1 = row == 0, row == zw - 1, lane < d, lane >= LANES - d
        hs = 0.5 * self.s

        def body(i):
            p = first + i * chunk
            r = self.base + p * zw
            b = self.get(B, r, n)
            bxp = self.get(B, r + zw, n)
            bxm = self.get(B, r - zw, n)
            bzp = jnp.where(z1, 0.0, self.get(B, r + 1, n))
            bzm = jnp.where(z0, 0.0, self.get(B, r - 1, n))
            byp = jnp.where(y1, 0.0, pltpu.roll(b, LANES - d, 1))
            bym = jnp.where(y0, 0.0, pltpu.roll(b, d, 1))
            dg = self.get(A, r, n) + hs * (6.0 * b + bxp + bxm + bzp + bzm + byp + bym)
            w = OMEGA / dg
            if valid is not None:
                w = jnp.where(valid(p), w, 0.0)
            self.put(A, r, dg)
            self.put(W, r, w)
            self.put(U, r, w * self.get(F, r, n))
            self.put(CX, r, hs * (b + bxp))
            self.put(CZ, r, jnp.where(z1, 0.0, hs * (b + bzp)))
            self.put(CY, r, jnp.where(y1, 0.0, hs * (b + byp)))

        assert count % chunk == 0
        each(count // chunk, n, body)

    def first_cx(self, plane):
        r = self.base + plane * self.zw
        n = self.zw
        self.put(CX, r, (0.5 * self.s) * (self.get(B, r, n) + self.get(B, r + n, n)))

    def around(self, q, r, n):
        zw, d = self.zw, self.d
        v = self.get(q, r, n)
        t = self.get(CX, r, n) * self.get(q, r + zw, n)
        t = t + self.get(CX, r - zw, n) * self.get(q, r - zw, n)
        t = t + self.get(CZ, r, n) * self.get(q, r + 1, n)
        t = t + self.get(CZ, r - 1, n) * self.get(q, r - 1, n)
        cy = self.get(CY, r, n)
        t = t + cy * pltpu.roll(v, LANES - d, 1)
        t = t + pltpu.roll(cy * v, d, 1)
        return v, t

    def sweep(self, src, dst, first, count, chunk):
        n = chunk * self.zw

        def body(i):
            r = self.base + (first + i * chunk) * self.zw
            v, t = self.around(src, r, n)
            self.put(dst, r, (1.0 - OMEGA) * v + self.get(W, r, n) * (self.get(F, r, n) + t))

        assert count % chunk == 0
        each(count // chunk, n, body)

    def residual(self, q, r, n):
        v, t = self.around(q, r, n)
        return self.get(F, r, n) + t - self.get(A, r, n) * v


def lane_pairs(t, d):
    s = t + pltpu.roll(t, LANES - d, 1)
    lane = lax.broadcasted_iota(jnp.int32, t.shape, 1)
    return jnp.where((lane // d) % 2 == 0, s, pltpu.roll(s, d, 1))


def restrict_planes(get, fine, first, pairs, coarse, q, plane, tmp, per):
    zw = fine.zw
    half = zw // 2

    def body(i):
        r = fine.base + (first + 2 * i * per) * zw
        t0 = i * per * zw if short(pairs // per, 2 * per * zw) else 0
        for k in range(per):
            v = get(r + 2 * k * zw, 2 * zw)
            tmp[pl.ds(t0 + k * zw, zw), :] = v[:zw] + v[zw:]
        t = tmp[pl.ds(t0, per * half, 2), :] + tmp[pl.ds(t0 + 1, per * half, 2), :]
        coarse.put(q, coarse.base + plane * half + i * per * half, lane_pairs(t, fine.d) * 0.125)

    assert pairs % per == 0
    each(pairs // per, 2 * per * zw, body)


def restrict_small(value, fine, coarse, q, tmp, count):
    zw, zc = fine.zw, coarse.zw
    tmp[pl.ds(0, count * 2 * zw), :] = value
    for z in range(zc):
        t = None
        for dx in range(2):
            for dz in range(2):
                part = tmp[pl.ds(dx * zw + 2 * z + dz, count, 2 * zw), :]
                t = part if t is None else t + part
        t = lane_pairs(t, fine.d) * 0.125
        if zc == 1:
            coarse.put(q, coarse.base, t)
        else:
            coarse.ref[q, pl.ds(coarse.base + z, count, zc), :] = t


def prolong_small(coarse, q, fine, p, tmp, count):
    zw, zc = fine.zw, coarse.zw
    for z in range(zc):
        v = coarse.get(q, coarse.base, count) if zc == 1 else coarse.ref[q, pl.ds(coarse.base + z, count, zc), :]
        for dx in range(2):
            for dz in range(2):
                tmp[pl.ds(dx * zw + 2 * z + dz, count, 2 * zw), :] = v
    n = count * 2 * zw
    fine.put(p, fine.base, fine.get(p, fine.base, n) + tmp[pl.ds(0, n), :])


def prolong_planes(coarse, q, plane, count, fine, src, dst, first, tmp, per=1):
    zw = fine.zw
    half = zw // 2

    def body(i):
        v = coarse.get(q, coarse.base + (plane + i * per) * half, per * half)
        t0 = i * per * zw if short(count // per, 2 * per * zw) else 0
        tmp[pl.ds(t0, per * half, 2), :] = v
        tmp[pl.ds(t0 + 1, per * half, 2), :] = v
        for k in range(per):
            e = tmp[pl.ds(t0 + k * zw, zw), :]
            r = fine.base + (first + 2 * (i * per + k)) * zw
            fine.put(dst, r, fine.get(src, r, zw) + e)
            fine.put(dst, r + zw, fine.get(src, r + zw, zw) + e)

    assert count % per == 0
    each(count // per, 2 * per * zw, body)


def keep(level, q, first, count, dst, k, sem):
    src = level.ref.at[q, pl.ds(first * level.zw, count * level.zw)]
    copy = pltpu.make_async_copy(src, dst.at[k], sem.at[k])
    copy.start()
    return copy


def pack_kernel(bx, bz, rhs, alpha, beta, even, odd, sem):
    up = 1 - lax.axis_index("wide") % 2
    waits = []
    at = 0
    for q, (src, size) in enumerate(((rhs, H - 1), (alpha, H - 1), (beta, H))):
        for k, dst in enumerate((even, odd)):
            upper = up if k == 0 else 1 - up
            start = pl.multiple_of(upper * ((bx - size) * bz), 8)
            copy = pltpu.make_async_copy(
                src.at[pl.ds(start, size * bz)], dst.at[pl.ds(at * bz, size * bz)], sem.at[2 * q + k]
            )
            copy.start()
            waits.append(copy)
        at += size
    for copy in waits:
        copy.wait()


def down_kernel(
    bx, bz, n_wide, n_narrow, own, even, odd, other, others, packed, ueven, uodd, keep0, keep1, lev0, lev1, part, tmp, sem0, sem1
):
    zw = bz * n_narrow
    planes = bx + 2 * H
    wide = lax.axis_index("wide")
    narrow = lax.axis_index("narrow")
    up = 1 - wide % 2
    l0 = Level(lev0, zw, 0)
    l1 = Level(lev1, zw // 2, 1)

    def place(q, src, src_plane, count, plane, z):
        def body(i):
            r = pl.multiple_of((plane + i) * zw + z, 8)
            l0.put(q, r, src[pl.ds((src_plane + i) * bz, bz), :])

        each(count, bz, body)

    g = H - 1
    all_h = 2 * g + H
    for index, (q, at, size) in enumerate(((F, 0, g), (A, g, g), (B, 2 * g, H))):
        above, below = H + bx, H - size
        p_even = up * above + (1 - up) * below
        p_odd = (1 - up) * above + up * below
        place(q, own, index * bx, bx, H, narrow * bz)
        place(q, even, at, size, p_even, narrow * bz)
        place(q, odd, at, size, p_odd, narrow * bz)
        for k in range(n_narrow - 1):
            z = (1 - narrow if n_narrow == 2 else lax.rem(narrow + 1 + k, n_narrow)) * bz
            place(q, other, (3 * k + index) * bx, bx, H, z)
            place(q, others, 2 * k * all_h + at, size, p_even, z)
            place(q, others, (2 * k + 1) * all_h + at, size, p_odd, z)
    first0, count0 = H - 2, bx + 4
    p1 = bx // 2 + 2 * H1
    waits = [keep(l0, F, first0, count0, keep0, F, sem0)]

    def valid0(p):
        x = wide * bx - H + p
        return jnp.logical_and(x >= 0, x < n_wide * bx)

    restrict_planes(lambda r, n: l0.get(B, r, n), l0, 1, p1, l1, B, 0, tmp.at[0], 1)
    restrict_planes(lambda r, n: l0.get(A, r, n), l0, 3, p1 - 2, l1, A, 1, tmp.at[1], 1)
    l0.first_cx(0)
    l0.setup(1, planes - 2, 1, valid0)
    waits += [keep(l0, q, first0, count0, keep0, q, sem0) for q in (W, CX, CZ, CY)]
    l0.sweep(U, V, 2, planes - 4, 1)
    waits.append(keep(l0, V, first0, count0, keep0, U, sem0))
    restrict_planes(lambda r, n: l0.residual(V, r, n), l0, 3, p1 - 2, l1, F, 1, tmp.at[2], 1)

    def valid1(p):
        x = wide * (bx // 2) - H1 + p
        return jnp.logical_and(x >= 0, x < n_wide * (bx // 2))

    k2 = bx // 4
    z2 = zw // 4
    n2 = k2 * z2
    l2 = Level(part, z2, 2)
    restrict_planes(lambda r, n: l1.get(A, r, n), l1, H1, k2, l2, 1, 0, tmp.at[1], 1)
    restrict_planes(lambda r, n: l1.get(B, r, n), l1, H1, k2, l2, 2, 0, tmp.at[0], 1)
    l1.first_cx(0)
    l1.put(CZ, 0, jnp.zeros((l1.zw, LANES), jnp.float32))
    l1.setup(1, p1 - 2, 1, valid1)
    waits += [keep(l1, q, 0, p1, keep1, q, sem1) for q in (F, W, CX, CZ, CY)]
    l1.sweep(U, V, 2, p1 - 4, 1)
    waits.append(keep(l1, V, 0, p1, keep1, U, sem1))
    n1 = 2 * l1.zw
    upper, lower = H1 + bx // 2 - 3, H1 + 1
    ueven[...] = l1.get(V, pl.multiple_of((up * upper + (1 - up) * lower) * l1.zw, 8), n1)
    uodd[...] = l1.get(V, pl.multiple_of(((1 - up) * upper + up * lower) * l1.zw, 8), n1)
    restrict_planes(lambda r, n: l1.residual(V, r, n), l1, H1, k2, l2, 0, 0, tmp.at[2], 1)
    which = lax.broadcasted_iota(jnp.int32, (n2, LANES), 1) % 4
    part[0] = jnp.where(which == 0, part[0], jnp.where(which == 1, part[1], part[2]))
    share = n2 // n_narrow
    mine = part[0, pl.ds(pl.multiple_of(narrow * share, 8), share), :]

    def spread(i):
        packed[pl.ds(i * share, share), :] = mine

    each(n_wide * n_narrow, share, spread)
    for copy in waits:
        copy.wait()


def margin(zl, index):
    return max(8, (4 if index == 2 else 2) * zl)


def up_kernel(
    bx, bz, n_wide, n_narrow, gathered, heven, hodd, keep0, keep1, out, lev2, lev3, lev4, lev5, lev0, lev1, near2, near3, tmp, sem0, sem1
):
    wide = lax.axis_index("wide")
    narrow = lax.axis_index("narrow")
    zw = bz * n_narrow
    fetch = []
    z1 = zw // 2
    for kept, lev, done, r in ((keep1, lev1, sem1, z1), (keep0, lev0, sem0, 0)):
        for q in range(KEPT):
            copy = pltpu.make_async_copy(kept.at[q], lev.at[q, pl.ds(r, kept.shape[1])], done.at[q])
            copy.start()
            fetch.append(copy)
    levels = []
    for index, ref in enumerate((lev2, lev3, lev4, lev5), 2):
        zl = zw // 2**index
        m = margin(zl, index)
        level = Level(ref, zl, index, m)
        level.nx = n_wide * bx // 2**index
        levels.append(level)
        zero = jnp.zeros((m, LANES), jnp.float32)
        for q in (F, W, CX, CZ, CY, U, B):
            level.put(q, 0, zero)
            level.put(q, m + level.nx * zl, zero)
    l2, l3, l4, l5 = levels
    planes2 = bx // 4
    n2 = planes2 * l2.zw
    n = n2 // n_narrow
    lane = lax.broadcasted_iota(jnp.int32, (n, LANES), 1) % 4

    def unpack(i):
        p = gathered[pl.ds(i * n, n), :]
        for q, k, first, second in ((F, 0, 1, 2), (A, 1, LANES - 1, 2), (B, 2, 1, LANES - 2)):
            t = jnp.where(lane == k, p, 0.0)
            t = t + pltpu.roll(t, first, 1)
            t = t + pltpu.roll(t, second, 1)
            l2.put(q, l2.base + i * n, t)

    each(n_wide * n_narrow, n, unpack)

    def chunk_of(level):
        return max(1, min(32 // level.zw, level.nx))

    def down(level, coarse, q, get, t):
        if level.zw >= 8:
            restrict_planes(get, level, 0, coarse.nx, coarse, q, 0, t, max(1, 16 // level.zw))
        else:
            restrict_small(get(level.base, level.nx * level.zw), level, coarse, q, t, coarse.nx)

    for level, coarse in ((l2, l3), (l3, l4), (l4, l5)):
        down(level, coarse, A, lambda r, m, level=level: level.get(A, r, m), tmp.at[0])
        down(level, coarse, B, lambda r, m, level=level: level.get(B, r, m), tmp.at[1])
    for level, coarse in ((l2, l3), (l3, l4), (l4, l5)):
        level.setup(0, level.nx, chunk_of(level))
        level.sweep(U, B, 0, level.nx, chunk_of(level))
        down(level, coarse, F, lambda r, m, level=level: level.residual(B, r, m), tmp.at[0])
    l5.setup(0, l5.nx, chunk_of(l5))
    src, dst = U, B
    for _ in range(BOTTOM - 1):
        l5.sweep(src, dst, 0, l5.nx, chunk_of(l5))
        src, dst = dst, src
    coarse = l5
    for level in (l4, l3):
        if level.zw >= 8:
            prolong_planes(coarse, src, 0, coarse.nx, level, B, B, 0, tmp.at[0], max(1, 16 // level.zw))
        else:
            prolong_small(coarse, src, level, B, tmp.at[0], coarse.nx)
        level.sweep(B, U, 0, level.nx, chunk_of(level))
        level.sweep(U, B, 0, level.nx, chunk_of(level))
        coarse, src = level, B
    start = wide * planes2
    w2 = Level(near2, l2.zw, 2)
    w3 = Level(near3, l3.zw, 3)

    def window(src, q, dst, k, first, count):
        n = count * src.zw
        dst.put(k, 0, src.get(q, pl.multiple_of(src.base + first * src.zw, 8), n))

    window(l3, B, w3, 0, start // 2 - 2, planes2 // 2 + 4)
    for q in (F, W, CX, CZ, CY):
        window(l2, q, w2, q, start - 4, planes2 + 8)
    window(l2, B, w2, U, start - 4, planes2 + 8)
    prolong_planes(w3, 0, 0, planes2 // 2 + 4, w2, U, U, 0, tmp.at[1], 2 if l2.zw < 16 else 1)
    w2.sweep(U, KEPT, 1, planes2 + 6, 2)
    w2.sweep(KEPT, U, 2, planes2 + 4, 2)
    for copy in fetch:
        copy.wait()
    l1 = Level(lev1, z1, 1)
    count1 = bx // 2 + 2 * H1 + 2
    up = 1 - wide % 2
    above, below = H1 + bx // 2 + 2, 1
    l1.put(U, pl.multiple_of((up * above + (1 - up) * below) * z1, 8), heven[...])
    l1.put(U, pl.multiple_of(((1 - up) * above + up * below) * z1, 8), hodd[...])
    prolong_planes(w2, U, 2, count1 // 2, l1, U, U, 0, tmp.at[0])
    l1.sweep(U, KEPT, 2, count1 - 4, 1)
    l1.sweep(KEPT, U, 3, count1 - 6, 1)
    l0 = Level(lev0, zw, 0)
    prolong_planes(l1, U, 3, bx // 2 + 2, l0, U, U, 0, tmp.at[1])
    l0.sweep(U, KEPT, 1, bx + 2, 1)
    l0.sweep(KEPT, U, 2, bx, 1)

    def give(i):
        r = pl.multiple_of((2 + i) * zw + narrow * bz, 8)
        out[pl.ds(i * bz, bz), :] = l0.get(U, r, bz)

    each(bx, bz, give)


def swap(array, axis, bit):
    n = lax.axis_size(axis)
    return lax.ppermute(array, axis, [(i, i ^ (1 << bit)) for i in range(n)])


def swap_odd(array):
    n = lax.axis_size("wide")
    pairs = [(i, i + 1) for i in range(1, n - 1, 2)]
    return lax.ppermute(array, "wide", pairs + [(j, i) for i, j in pairs])


def from_others(array):
    n = lax.axis_size("narrow")
    if n == 2:
        return swap(array, "narrow", 0)
    return jnp.concatenate(
        [lax.ppermute(array, "narrow", [((i + k) % n, i) for i in range(n)]) for k in range(1, n)]
    )


def shards(n_wide, n_narrow, rhs, alpha, beta):
    bx, bz, lanes = rhs.shape
    flat = lambda t: t.reshape(-1, lanes)
    zw = bz * n_narrow
    f32 = jnp.float32
    planes, p1 = bx + 2 * H, bx // 2 + 2 * H1
    n2 = (bx // 4) * (zw // 4)
    vmem, hbm = pl.BlockSpec(memory_space=pltpu.VMEM), pl.BlockSpec(memory_space=pl.ANY)
    keep0 = jax.ShapeDtypeStruct((KEPT, (bx + 4) * zw, lanes), f32)
    keep1 = jax.ShapeDtypeStruct((KEPT, p1 * (zw // 2), lanes), f32)
    u_face = jax.ShapeDtypeStruct((zw, lanes), f32)
    sems = [pltpu.SemaphoreType.DMA((KEPT,)), pltpu.SemaphoreType.DMA((KEPT,))]

    def params(scratch, rows):
        size = 4 * sum(math.prod(t.shape) for t in scratch[:-2]) + 4 * lanes * rows
        return pltpu.CompilerParams(vmem_limit_bytes=min(255 * 2**18, size + size // 8 + 2**21))

    face = jax.ShapeDtypeStruct(((3 * H - 2) * bz, lanes), f32)
    even, odd = pl.pallas_call(
        functools.partial(pack_kernel, bx, bz),
        out_shape=[face, face],
        in_specs=[pl.BlockSpec(memory_space=pltpu.HBM)] * 3,
        out_specs=[vmem] * 2,
        scratch_shapes=[pltpu.SemaphoreType.DMA((6,))],
        compiler_params=pltpu.CompilerParams(vmem_limit_bytes=62 * 2**20),
        name="pack",
    )(flat(rhs), flat(alpha), flat(beta))
    even, odd, rhs, alpha, beta = lax.optimization_barrier((even, odd, rhs, alpha, beta))
    own = jnp.concatenate([flat(rhs), flat(alpha), flat(beta)])
    even = swap(even, "wide", 0)
    odd = swap_odd(odd)
    other = from_others(own)
    others = from_others(jnp.concatenate([even, odd]))
    scratch = [
        pltpu.VMEM((9, planes * zw, lanes), f32),
        pltpu.VMEM((9, p1 * (zw // 2), lanes), f32),
        pltpu.VMEM((3, n2, lanes), f32),
        pltpu.VMEM((3, p1 * zw, lanes), f32),
        *sems,
    ]
    packed, ueven, uodd, keep0, keep1 = pl.pallas_call(
        functools.partial(down_kernel, bx, bz, n_wide, n_narrow),
        out_shape=[jax.ShapeDtypeStruct((n_wide * n2, lanes), f32), u_face, u_face, keep0, keep1],
        in_specs=[vmem] * 5,
        out_specs=[vmem, vmem, vmem, hbm, hbm],
        scratch_shapes=scratch,
        compiler_params=params(scratch, 3 * planes * zw),
        name="down",
    )(own, even, odd, other, others)
    heven, hodd = swap(ueven, "wide", 0), swap_odd(uodd)
    gathered = lax.all_to_all(packed, ("wide", "narrow"), 0, 0, tiled=True)
    nx = n_wide * bx
    scratch = []
    for index in range(2, LEVELS):
        zl = zw // 2**index
        scratch.append(pltpu.VMEM((8, nx // 2**index * zl + 2 * margin(zl, index), lanes), f32))
    scratch += [
        pltpu.VMEM((KEPT + 1, *keep0.shape[1:]), f32),
        pltpu.VMEM((KEPT + 1, (p1 + 2) * (zw // 2), lanes), f32),
        pltpu.VMEM((KEPT + 1, (bx // 4 + 8) * (zw // 4), lanes), f32),
        pltpu.VMEM((1, (bx // 8 + 4) * (zw // 8), lanes), f32),
        pltpu.VMEM((2, LONGEST // 2, lanes), f32),
        *sems,
    ]
    out = pl.pallas_call(
        functools.partial(up_kernel, bx, bz, n_wide, n_narrow),
        out_shape=jax.ShapeDtypeStruct((bx * bz, lanes), f32),
        in_specs=[vmem, vmem, vmem, hbm, hbm],
        out_specs=vmem,
        scratch_shapes=scratch,
        compiler_params=params(scratch, bx * bz + n_wide * n2 + 2 * zw),
        name="up",
    )(gathered, heven, hodd, keep0, keep1)
    return out.reshape(bx, bz, lanes)


def solution(mesh):
    n_wide, n_narrow = mesh.shape["wide"], mesh.shape["narrow"]
    spec = P("wide", "narrow", None)
    return jax.shard_map(
        functools.partial(shards, n_wide, n_narrow),
        mesh=mesh,
        in_specs=(spec, spec, spec),
        out_specs=spec,
        check_vma=False,
    )
```

```python
import functools
import math

import jax
import jax.numpy as jnp
from jax import lax
from jax.experimental import pallas as pl
from jax.experimental.pallas import tpu as pltpu
from jax.sharding import PartitionSpec as P

LEVELS = 6
BOTTOM = 6
OMEGA = 2.0 / 3.0
LANES = 128
H1 = 3
H = 2 * H1 + 1
LONGEST = 2048


def short(n, rows):
    return n * rows <= LONGEST


def each(n, rows, body):
    if short(n, rows):
        for i in range(n):
            body(i)
    else:

        def step(i, _):
            body(i)
            return 0

        lax.fori_loop(0, n, step, 0)


F, W, CX, CZ, CY, U, A, B, V = range(9)
KEPT = 6


class Level:
    def __init__(self, ref, zw, index, base=0):
        self.ref, self.zw, self.base = ref, zw, base
        self.d, self.s = 2**index, 0.25**index

    def at(self, plane):
        return Level.moved(self, self.base + plane * self.zw)

    def moved(self, base):
        other = Level(self.ref, self.zw, 0, base)
        other.d, other.s = self.d, self.s
        return other

    def get(self, q, r, n):
        return self.ref[q, pl.ds(r, n), :]

    def put(self, q, r, value):
        self.ref[q, pl.ds(r, value.shape[0]), :] = value

    def setup(self, first, count, chunk, valid=None):
        zw, d = self.zw, self.d
        n = chunk * zw
        row = lax.broadcasted_iota(jnp.int32, (n, LANES), 0) % zw
        lane = lax.broadcasted_iota(jnp.int32, (n, LANES), 1)
        z0, z1, y0, y1 = row == 0, row == zw - 1, lane < d, lane >= LANES - d
        hs = 0.5 * self.s

        def body(i):
            p = first + i * chunk
            r = self.base + p * zw
            b = self.get(B, r, n)
            bxp = self.get(B, r + zw, n)
            bxm = self.get(B, r - zw, n)
            bzp = jnp.where(z1, 0.0, self.get(B, r + 1, n))
            bzm = jnp.where(z0, 0.0, self.get(B, r - 1, n))
            byp = jnp.where(y1, 0.0, pltpu.roll(b, LANES - d, 1))
            bym = jnp.where(y0, 0.0, pltpu.roll(b, d, 1))
            dg = self.get(A, r, n) + hs * (6.0 * b + bxp + bxm + bzp + bzm + byp + bym)
            w = OMEGA / dg
            if valid is not None:
                w = jnp.where(valid(p), w, 0.0)
            self.put(A, r, dg)
            self.put(W, r, w)
            self.put(U, r, w * self.get(F, r, n))
            self.put(CX, r, hs * (b + bxp))
            self.put(CZ, r, jnp.where(z1, 0.0, hs * (b + bzp)))
            self.put(CY, r, jnp.where(y1, 0.0, hs * (b + byp)))

        assert count % chunk == 0
        each(count // chunk, n, body)

    def first_cx(self, plane):
        r = self.base + plane * self.zw
        n = self.zw
        self.put(CX, r, (0.5 * self.s) * (self.get(B, r, n) + self.get(B, r + n, n)))

    def around(self, q, r, n):
        zw, d = self.zw, self.d
        v = self.get(q, r, n)
        t = self.get(CX, r, n) * self.get(q, r + zw, n)
        t = t + self.get(CX, r - zw, n) * self.get(q, r - zw, n)
        t = t + self.get(CZ, r, n) * self.get(q, r + 1, n)
        t = t + self.get(CZ, r - 1, n) * self.get(q, r - 1, n)
        cy = self.get(CY, r, n)
        t = t + cy * pltpu.roll(v, LANES - d, 1)
        t = t + pltpu.roll(cy * v, d, 1)
        return v, t

    def sweep(self, src, dst, first, count, chunk):
        n = chunk * self.zw

        def body(i):
            r = self.base + (first + i * chunk) * self.zw
            v, t = self.around(src, r, n)
            self.put(dst, r, (1.0 - OMEGA) * v + self.get(W, r, n) * (self.get(F, r, n) + t))

        assert count % chunk == 0
        each(count // chunk, n, body)

    def residual(self, q, r, n):
        v, t = self.around(q, r, n)
        return self.get(F, r, n) + t - self.get(A, r, n) * v


def lane_pairs(t, d):
    s = t + pltpu.roll(t, LANES - d, 1)
    lane = lax.broadcasted_iota(jnp.int32, t.shape, 1)
    return jnp.where((lane // d) % 2 == 0, s, pltpu.roll(s, d, 1))


def restrict_planes(get, fine, first, pairs, coarse, q, plane, tmp, per):
    zw = fine.zw
    half = zw // 2

    def body(i):
        r = fine.base + (first + 2 * i * per) * zw
        t0 = i * per * zw if short(pairs // per, 2 * per * zw) else 0
        for k in range(per):
            v = get(r + 2 * k * zw, 2 * zw)
            tmp[pl.ds(t0 + k * zw, zw), :] = v[:zw] + v[zw:]
        t = tmp[pl.ds(t0, per * half, 2), :] + tmp[pl.ds(t0 + 1, per * half, 2), :]
        coarse.put(q, coarse.base + plane * half + i * per * half, lane_pairs(t, fine.d) * 0.125)

    assert pairs % per == 0
    each(pairs // per, 2 * per * zw, body)


def restrict_small(value, fine, coarse, q, tmp, count):
    zw, zc = fine.zw, coarse.zw
    tmp[pl.ds(0, count * 2 * zw), :] = value
    for z in range(zc):
        t = None
        for dx in range(2):
            for dz in range(2):
                part = tmp[pl.ds(dx * zw + 2 * z + dz, count, 2 * zw), :]
                t = part if t is None else t + part
        t = lane_pairs(t, fine.d) * 0.125
        if zc == 1:
            coarse.put(q, coarse.base, t)
        else:
            coarse.ref[q, pl.ds(coarse.base + z, count, zc), :] = t


def prolong_small(coarse, q, fine, p, tmp, count):
    zw, zc = fine.zw, coarse.zw
    for z in range(zc):
        v = coarse.get(q, coarse.base, count) if zc == 1 else coarse.ref[q, pl.ds(coarse.base + z, count, zc), :]
        for dx in range(2):
            for dz in range(2):
                tmp[pl.ds(dx * zw + 2 * z + dz, count, 2 * zw), :] = v
    n = count * 2 * zw
    fine.put(p, fine.base, fine.get(p, fine.base, n) + tmp[pl.ds(0, n), :])


def prolong_planes(coarse, q, plane, count, fine, src, dst, first, tmp, per=1):
    zw = fine.zw
    half = zw // 2

    def body(i):
        v = coarse.get(q, coarse.base + (plane + i * per) * half, per * half)
        t0 = i * per * zw if short(count // per, 2 * per * zw) else 0
        tmp[pl.ds(t0, per * half, 2), :] = v
        tmp[pl.ds(t0 + 1, per * half, 2), :] = v
        for k in range(per):
            e = tmp[pl.ds(t0 + k * zw, zw), :]
            r = fine.base + (first + 2 * (i * per + k)) * zw
            fine.put(dst, r, fine.get(src, r, zw) + e)
            fine.put(dst, r + zw, fine.get(src, r + zw, zw) + e)

    assert count % per == 0
    each(count // per, 2 * per * zw, body)


def keep(level, q, first, count, dst, k, sem):
    src = level.ref.at[q, pl.ds(first * level.zw, count * level.zw)]
    copy = pltpu.make_async_copy(src, dst.at[k], sem.at[k])
    copy.start()
    return copy


def pack_kernel(bx, bz, rhs, alpha, beta, even, odd, sem):
    up = 1 - lax.axis_index("wide") % 2
    waits = []
    at = 0
    for q, (src, size) in enumerate(((rhs, H - 1), (alpha, H - 1), (beta, H))):
        for k, dst in enumerate((even, odd)):
            upper = up if k == 0 else 1 - up
            start = pl.multiple_of(upper * ((bx - size) * bz), 8)
            copy = pltpu.make_async_copy(
                src.at[pl.ds(start, size * bz)], dst.at[pl.ds(at * bz, size * bz)], sem.at[2 * q + k]
            )
            copy.start()
            waits.append(copy)
        at += size
    for copy in waits:
        copy.wait()


def spread4(p, lane, k):
    t = jnp.where(lane == k, p, 0.0)
    t = t + pltpu.roll(t, 1 if k % 2 == 0 else LANES - 1, 1)
    return t + pltpu.roll(t, 2 if k < 2 else LANES - 2, 1)


def down_kernel(
    bx, bz, n_wide, n_narrow, own, even, odd, other, others, packed, ueven, uodd, keep0, keep1, lev0, lev1, part, tmp, sem0, sem1
):
    zw = bz * n_narrow
    planes = bx + 2 * H
    wide = lax.axis_index("wide")
    narrow = lax.axis_index("narrow")
    up = 1 - wide % 2
    l0 = Level(lev0, zw, 0)
    l1 = Level(lev1, zw // 2, 1)

    def place(q, src, src_plane, count, plane, z):
        def body(i):
            r = pl.multiple_of((plane + i) * zw + z, 8)
            l0.put(q, r, src[pl.ds((src_plane + i) * bz, bz), :])

        each(count, bz, body)

    g = H - 1
    all_h = 2 * g + H
    for index, (q, at, size) in enumerate(((F, 0, g), (A, g, g), (B, 2 * g, H))):
        above, below = H + bx, H - size
        p_even = up * above + (1 - up) * below
        p_odd = (1 - up) * above + up * below
        place(q, own, index * bx, bx, H, narrow * bz)
        place(q, even, at, size, p_even, narrow * bz)
        place(q, odd, at, size, p_odd, narrow * bz)
        for k in range(n_narrow - 1):
            z = (1 - narrow if n_narrow == 2 else lax.rem(narrow + 1 + k, n_narrow)) * bz
            place(q, other, (3 * k + index) * bx, bx, H, z)
            place(q, others, 2 * k * all_h + at, size, p_even, z)
            place(q, others, (2 * k + 1) * all_h + at, size, p_odd, z)
    first0, count0 = H - 2, bx + 4
    p1 = bx // 2 + 2 * H1
    waits = [keep(l0, F, first0, count0, keep0, F, sem0)]

    def valid0(p):
        x = wide * bx - H + p
        return jnp.logical_and(x >= 0, x < n_wide * bx)

    restrict_planes(lambda r, n: l0.get(B, r, n), l0, 1, p1, l1, B, 0, tmp.at[0], 1)
    restrict_planes(lambda r, n: l0.get(A, r, n), l0, 3, p1 - 2, l1, A, 1, tmp.at[1], 1)
    l0.first_cx(0)
    l0.setup(1, planes - 2, 1, valid0)
    waits += [keep(l0, q, first0, count0, keep0, q, sem0) for q in (W, CX, CZ, CY)]
    l0.sweep(U, V, 2, planes - 4, 1)
    waits.append(keep(l0, V, first0, count0, keep0, U, sem0))
    restrict_planes(lambda r, n: l0.residual(V, r, n), l0, 3, p1 - 2, l1, F, 1, tmp.at[2], 1)

    def valid1(p):
        x = wide * (bx // 2) - H1 + p
        return jnp.logical_and(x >= 0, x < n_wide * (bx // 2))

    k2 = bx // 4
    z2 = zw // 4
    n2 = k2 * z2
    l2 = Level(part, z2, 2)
    restrict_planes(lambda r, n: l1.get(A, r, n), l1, H1, k2, l2, 1, 0, tmp.at[1], 1)
    restrict_planes(lambda r, n: l1.get(B, r, n), l1, H1, k2, l2, 2, 0, tmp.at[0], 1)
    l1.first_cx(0)
    l1.put(CZ, 0, jnp.zeros((l1.zw, LANES), jnp.float32))
    l1.setup(1, p1 - 2, 1, valid1)
    waits += [keep(l1, q, 0, p1, keep1, q, sem1) for q in (F, W, CX, CZ, CY)]
    l1.sweep(U, V, 2, p1 - 4, 1)
    waits.append(keep(l1, V, 0, p1, keep1, U, sem1))
    n1 = 2 * l1.zw
    upper, lower = H1 + bx // 2 - 3, H1 + 1
    above, below = l1.get(V, upper * l1.zw, n1), l1.get(V, lower * l1.zw, n1)
    ueven[...] = jnp.where(up == 1, above, below)
    uodd[...] = jnp.where(up == 1, below, above)
    restrict_planes(lambda r, n: l1.residual(V, r, n), l1, H1, k2, l2, 0, 0, tmp.at[2], 1)
    which = lax.broadcasted_iota(jnp.int32, (z2, LANES), 1) % 4
    fs, as_, bs = [[part[q, pl.ds(k * z2, z2), :] for k in range(4)] for q in range(3)]

    def four(p):
        return jnp.where(which == 0, p[0], jnp.where(which == 1, p[1], jnp.where(which == 2, p[2], p[3])))

    parts = [four(fs), four((as_[0], bs[0], as_[1], bs[1])), four((as_[2], bs[2], as_[3], bs[3]))]

    def spread(i):
        for k in range(3):
            packed[pl.ds((3 * i + k) * z2, z2), :] = parts[k]

    each(n_wide, 3 * z2, spread)
    for copy in waits:
        copy.wait()


def margin(zl, index):
    return max(8, (4 if index == 2 else 2) * zl)


def up_kernel(
    bx, bz, n_wide, n_narrow, gathered, heven, hodd, keep0, keep1, out, lev2, lev3, lev4, lev5, lev0, lev1, near2, near3, tmp, sem0, sem1
):
    wide = lax.axis_index("wide")
    narrow = lax.axis_index("narrow")
    zw = bz * n_narrow
    fetch = []
    z1 = zw // 2
    for kept, lev, done, r in ((keep1, lev1, sem1, z1), (keep0, lev0, sem0, 0)):
        for q in range(KEPT):
            copy = pltpu.make_async_copy(kept.at[q], lev.at[q, pl.ds(r, kept.shape[1])], done.at[q])
            copy.start()
            fetch.append(copy)
    levels = []
    for index, ref in enumerate((lev2, lev3, lev4, lev5), 2):
        zl = zw // 2**index
        m = margin(zl, index)
        level = Level(ref, zl, index, m)
        level.nx = n_wide * bx // 2**index
        levels.append(level)
        zero = jnp.zeros((m, LANES), jnp.float32)
        for q in (F, W, CX, CZ, CY, U, B):
            level.put(q, 0, zero)
            level.put(q, m + level.nx * zl, zero)
    l2, l3, l4, l5 = levels
    planes2 = bx // 4
    z2 = l2.zw
    lane = lax.broadcasted_iota(jnp.int32, (z2, LANES), 1) % 4

    def unpack(w):
        r = l2.base + w * planes2 * z2
        for part, wanted in (
            (0, ((F, 0), (F, 1), (F, 2), (F, 3))),
            (1, ((A, 0), (B, 0), (A, 1), (B, 1))),
            (2, ((A, 2), (B, 2), (A, 3), (B, 3))),
        ):
            p = gathered[pl.ds((3 * w + part) * z2, z2), :]
            for k, (q, plane) in enumerate(wanted):
                l2.put(q, r + plane * z2, spread4(p, lane, k))

    each(n_wide, 12 * z2, unpack)

    def chunk_of(level):
        return max(1, min(32 // level.zw, level.nx))

    def down(level, coarse, q, get, t):
        if level.zw >= 8:
            restrict_planes(get, level, 0, coarse.nx, coarse, q, 0, t, max(1, 16 // level.zw))
        else:
            restrict_small(get(level.base, level.nx * level.zw), level, coarse, q, t, coarse.nx)

    for level, coarse in ((l2, l3), (l3, l4), (l4, l5)):
        down(level, coarse, A, lambda r, m, level=level: level.get(A, r, m), tmp.at[0])
        down(level, coarse, B, lambda r, m, level=level: level.get(B, r, m), tmp.at[1])
    for level, coarse in ((l2, l3), (l3, l4), (l4, l5)):
        level.setup(0, level.nx, chunk_of(level))
        level.sweep(U, B, 0, level.nx, chunk_of(level))
        down(level, coarse, F, lambda r, m, level=level: level.residual(B, r, m), tmp.at[0])
    l5.setup(0, l5.nx, chunk_of(l5))
    src, dst = U, B
    for _ in range(BOTTOM - 1):
        l5.sweep(src, dst, 0, l5.nx, chunk_of(l5))
        src, dst = dst, src
    coarse = l5
    for level in (l4, l3):
        if level.zw >= 8:
            prolong_planes(coarse, src, 0, coarse.nx, level, B, B, 0, tmp.at[0], max(1, 16 // level.zw))
        else:
            prolong_small(coarse, src, level, B, tmp.at[0], coarse.nx)
        level.sweep(B, U, 0, level.nx, chunk_of(level))
        level.sweep(U, B, 0, level.nx, chunk_of(level))
        coarse, src = level, B
    start = wide * planes2
    w2 = Level(near2, l2.zw, 2)
    w3 = Level(near3, l3.zw, 3)

    def window(src, q, dst, k, first, count):
        n = count * src.zw
        dst.put(k, 0, src.get(q, pl.multiple_of(src.base + first * src.zw, 8), n))

    window(l3, B, w3, 0, start // 2 - 2, planes2 // 2 + 4)
    for q in (F, W, CX, CZ, CY):
        window(l2, q, w2, q, start - 4, planes2 + 8)
    window(l2, B, w2, U, start - 4, planes2 + 8)
    prolong_planes(w3, 0, 0, planes2 // 2 + 4, w2, U, U, 0, tmp.at[1], 2 if l2.zw < 16 else 1)
    w2.sweep(U, KEPT, 1, planes2 + 6, 2)
    w2.sweep(KEPT, U, 2, planes2 + 4, 2)
    for copy in fetch:
        copy.wait()
    l1 = Level(lev1, z1, 1)
    count1 = bx // 2 + 2 * H1 + 2
    up = 1 - wide % 2
    above, below = H1 + bx // 2 + 2, 1
    l1.put(U, pl.multiple_of((up * above + (1 - up) * below) * z1, 8), heven[...])
    l1.put(U, pl.multiple_of(((1 - up) * above + up * below) * z1, 8), hodd[...])
    prolong_planes(w2, U, 2, count1 // 2, l1, U, U, 0, tmp.at[0])
    l1.sweep(U, KEPT, 2, count1 - 4, 1)
    l1.sweep(KEPT, U, 3, count1 - 6, 1)
    l0 = Level(lev0, zw, 0)
    prolong_planes(l1, U, 3, bx // 2 + 2, l0, U, U, 0, tmp.at[1])
    l0.sweep(U, KEPT, 1, bx + 2, 1)
    l0.sweep(KEPT, U, 2, bx, 1)

    def give(i):
        r = pl.multiple_of((2 + i) * zw + narrow * bz, 8)
        out[pl.ds(i * bz, bz), :] = l0.get(U, r, bz)

    each(bx, bz, give)


def swap(array, axis, bit):
    n = lax.axis_size(axis)
    return lax.ppermute(array, axis, [(i, i ^ (1 << bit)) for i in range(n)])


def swap_odd(array):
    n = lax.axis_size("wide")
    pairs = [(i, i + 1) for i in range(1, n - 1, 2)]
    return lax.ppermute(array, "wide", pairs + [(j, i) for i, j in pairs])


def from_others(array):
    n = lax.axis_size("narrow")
    if n == 2:
        return swap(array, "narrow", 0)
    return jnp.concatenate(
        [lax.ppermute(array, "narrow", [((i + k) % n, i) for i in range(n)]) for k in range(1, n)]
    )


def shards(n_wide, n_narrow, rhs, alpha, beta):
    bx, bz, lanes = rhs.shape
    flat = lambda t: t.reshape(-1, lanes)
    zw = bz * n_narrow
    f32 = jnp.float32
    planes, p1 = bx + 2 * H, bx // 2 + 2 * H1
    n2 = (bx // 4) * (zw // 4)
    vmem, hbm = pl.BlockSpec(memory_space=pltpu.VMEM), pl.BlockSpec(memory_space=pl.ANY)
    keep0 = jax.ShapeDtypeStruct((KEPT, (bx + 4) * zw, lanes), f32)
    keep1 = jax.ShapeDtypeStruct((KEPT, p1 * (zw // 2), lanes), f32)
    u_face = jax.ShapeDtypeStruct((zw, lanes), f32)
    sems = [pltpu.SemaphoreType.DMA((KEPT,)), pltpu.SemaphoreType.DMA((KEPT,))]

    def params(scratch, rows):
        size = 4 * sum(math.prod(t.shape) for t in scratch[:-2]) + 4 * lanes * rows
        return pltpu.CompilerParams(vmem_limit_bytes=min(255 * 2**18, size + size // 8 + 2**21))

    face = jax.ShapeDtypeStruct(((3 * H - 2) * bz, lanes), f32)
    even, odd = pl.pallas_call(
        functools.partial(pack_kernel, bx, bz),
        out_shape=[face, face],
        in_specs=[pl.BlockSpec(memory_space=pltpu.HBM)] * 3,
        out_specs=[vmem] * 2,
        scratch_shapes=[pltpu.SemaphoreType.DMA((6,))],
        compiler_params=pltpu.CompilerParams(vmem_limit_bytes=62 * 2**20),
        name="pack",
    )(flat(rhs), flat(alpha), flat(beta))
    even, odd, rhs, alpha, beta = lax.optimization_barrier((even, odd, rhs, alpha, beta))
    own = jnp.concatenate([flat(rhs), flat(alpha), flat(beta)])
    even = swap(even, "wide", 0)
    odd = swap_odd(odd)
    other = from_others(own)
    others = from_others(jnp.concatenate([even, odd]))
    scratch = [
        pltpu.VMEM((9, planes * zw, lanes), f32),
        pltpu.VMEM((9, p1 * (zw // 2), lanes), f32),
        pltpu.VMEM((3, n2, lanes), f32),
        pltpu.VMEM((3, p1 * zw, lanes), f32),
        *sems,
    ]
    packed, ueven, uodd, keep0, keep1 = pl.pallas_call(
        functools.partial(down_kernel, bx, bz, n_wide, n_narrow),
        out_shape=[jax.ShapeDtypeStruct((n_wide * 3 * (zw // 4), lanes), f32), u_face, u_face, keep0, keep1],
        in_specs=[vmem] * 5,
        out_specs=[vmem, vmem, vmem, hbm, hbm],
        scratch_shapes=scratch,
        compiler_params=params(scratch, 3 * planes * zw),
        name="down",
    )(own, even, odd, other, others)
    heven, hodd = swap(ueven, "wide", 0), swap_odd(uodd)
    gathered = lax.all_to_all(packed, "wide", 0, 0, tiled=True)
    nx = n_wide * bx
    scratch = []
    for index in range(2, LEVELS):
        zl = zw // 2**index
        scratch.append(pltpu.VMEM((8, nx // 2**index * zl + 2 * margin(zl, index), lanes), f32))
    scratch += [
        pltpu.VMEM((KEPT + 1, *keep0.shape[1:]), f32),
        pltpu.VMEM((KEPT + 1, (p1 + 2) * (zw // 2), lanes), f32),
        pltpu.VMEM((KEPT + 1, (bx // 4 + 8) * (zw // 4), lanes), f32),
        pltpu.VMEM((1, (bx // 8 + 4) * (zw // 8), lanes), f32),
        pltpu.VMEM((2, LONGEST // 2, lanes), f32),
        *sems,
    ]
    out = pl.pallas_call(
        functools.partial(up_kernel, bx, bz, n_wide, n_narrow),
        out_shape=jax.ShapeDtypeStruct((bx * bz, lanes), f32),
        in_specs=[vmem, vmem, vmem, hbm, hbm],
        out_specs=vmem,
        scratch_shapes=scratch,
        compiler_params=params(scratch, bx * bz + n_wide * n2 + 2 * zw),
        name="up",
    )(gathered, heven, hodd, keep0, keep1)
    return out.reshape(bx, bz, lanes)


def solution(mesh):
    n_wide, n_narrow = mesh.shape["wide"], mesh.shape["narrow"]
    spec = P("wide", "narrow", None)
    return jax.shard_map(
        functools.partial(shards, n_wide, n_narrow),
        mesh=mesh,
        in_specs=(spec, spec, spec),
        out_specs=spec,
        check_vma=False,
    )
```
